32 devices in a mesh: rows: 2 (over x), cols: 16 (over z, y, core).
Axes of the slice: x: 2, y: 2, z: 4, core: 2. Of those that a mesh axis runs over, the one named last changes fastest.
Arguments:
- plan: bfloat16 [4096, 8192], P('rows', 'cols'), may hold values from 0.049804688 to 20
- source: bfloat16 [4096, 512], P('rows', 'cols'), may hold values from -6 to 6
- target: bfloat16 [8192, 512], P('cols', 'rows'), may hold values from -6 to 6
- source_mass: float32 [4096], P('rows'), may hold values from 0.5 to 2
- target_mass: float32 [8192], P('cols'), may hold values from 0.5 to 2
Outputs:
- row_scaling: float32 [4096], P('rows')
- col_scaling: float32 [8192], P('cols')
The draws below stay inside these ranges and needn't reach their ends.
All inputs are finite; a program needn't handle non-finite values.
Results may differ from the reference program's by a relative error of at most 0.00089.
Values may be sent and summed in bfloat16 or wider, within the bound.
No kernel may reach another device: no remote copies, remote signals or barrier semaphores. Data moves between devices by JAX's collectives and lax.ppermute only.
A program may use at most 64 MiB of HBM per device.

```python
import math
import jax
import jax.numpy as jnp
from jax import lax

D = 512
COLS_DEV = 512
SOURCES = 4096
TARGETS = 8192
N_COLS = 16


def block_scale(key, shape, split, low, top_value):
    def one(position, blocks):
        draws = jax.random.uniform(jax.random.fold_in(jax.random.fold_in(key, 6), position), (blocks,), jnp.float32, low / len(split), top_value / len(split))
        return jnp.repeat(jnp.exp(draws), shape[position] // blocks).reshape((-1,) + (1,) * (len(shape) - position - 1))

    level = one(*split[0])
    for cut in split[1:]:
        level = level * one(*cut)
    return level


def centred(rng, shape, scale, limit, split=(), kind=jnp.bfloat16):
    factor_of = block_scale(rng, shape, split, -0.22, 0.18) if split else 1.0
    entries = jax.random.normal(rng, shape, jnp.float32) * scale * factor_of
    return jnp.minimum(jnp.maximum(entries, -limit), limit).astype(kind)


def setup_inputs(seed: int = 0) -> dict:
    arg_keys = jax.random.split(jax.random.key(seed), 6)
    plan = jnp.clip(jnp.exp(math.log(20.0) - 5.9953784 * jax.random.uniform(arg_keys[0], (SOURCES, TARGETS), jnp.float32) ** block_scale(arg_keys[0], (SOURCES, TARGETS), ((0, 2), (1, 16)), -0.2, 0.2)), 0.049804688, 20.0).astype(jnp.bfloat16)
    source = centred(arg_keys[1], (SOURCES, D), 1.0, 6.0, ((0, 2), (1, 16)))
    target = centred(arg_keys[2], (TARGETS, D), 1.0, 6.0, ((0, 16), (1, 2)))
    source_mass = jnp.clip(jnp.exp(math.log(2.0) - 1.3862944 * jax.random.uniform(arg_keys[3], (SOURCES,), jnp.float32) ** block_scale(arg_keys[3], (SOURCES,), ((0, 2),), -0.2, 0.2)), 0.5, 2.0)
    target_mass = jnp.clip(jnp.exp(math.log(2.0) - 1.3862944 * jax.random.uniform(arg_keys[4], (TARGETS,), jnp.float32) ** block_scale(arg_keys[4], (TARGETS,), ((0, 16),), -0.2, 0.2)), 0.5, 2.0)
    return {"plan": plan, "source": source, "target": target, "source_mass": source_mass, "target_mass": target_mass}


sharpness = 1.5

def unit_rows(matrix):
    values = matrix.astype(jnp.float32)
    return (values * lax.rsqrt(lax.optimization_barrier(jnp.sum(values * values, axis=1, keepdims=True)) + 1e-06)).astype(jnp.bfloat16)

def matmul(left, right):
    return jnp.dot(left.astype(jnp.float32), right.astype(jnp.float32), precision=lax.Precision.HIGHEST)

def reference(plan, source, target, source_mass, target_mass):
    sources_unit = unit_rows(source)
    targets_unit = unit_rows(target)
    blocks = jnp.arange(N_COLS, dtype=jnp.int32)

    def couple(running, block_index):
        start = (block_index * COLS_DEV).astype(jnp.int32)
        plan_block = lax.dynamic_slice_in_dim(plan, start, COLS_DEV, 1)
        target_block = lax.dynamic_slice_in_dim(targets_unit, start, COLS_DEV, 0)
        projected = matmul(plan_block, target_block).astype(jnp.bfloat16)
        return (running + matmul(sources_unit.T, projected), None)
    coupling, _ = lax.scan(couple, jnp.zeros((D, D), jnp.float32), blocks)
    normalized = (coupling * lax.rsqrt(jnp.sum(coupling * coupling) / 2048.0 + 1e-06)).astype(jnp.bfloat16)
    lifted = matmul(sources_unit, normalized).astype(jnp.bfloat16)

    def kernel_block(block_index):
        start = (block_index * COLS_DEV).astype(jnp.int32)
        target_block = lax.dynamic_slice_in_dim(targets_unit, start, COLS_DEV, 0)
        return jnp.exp(sharpness * matmul(lifted, target_block.T))
    col_scaling = jnp.ones((TARGETS,), jnp.float32)
    row_scaling = source_mass
    for repeat in range(2):
        col_blocks = col_scaling.reshape(N_COLS, COLS_DEV)

        def row_fold(running, block_index):
            return (running + jnp.dot(kernel_block(block_index), col_blocks[block_index], precision=lax.Precision.HIGHEST), None)
        row_totals, _ = lax.scan(row_fold, jnp.zeros((SOURCES,), jnp.float32), blocks)
        row_scaling = source_mass / (row_totals / TARGETS)
        col_totals = lax.map(lambda block_index: jnp.dot(row_scaling, kernel_block(block_index), precision=lax.Precision.HIGHEST), blocks)
        col_scaling = target_mass / (col_totals.reshape(TARGETS) / SOURCES)
    return (row_scaling, col_scaling)
```

```python
import functools

import jax
import jax.numpy as jnp
from jax import lax
from jax.experimental import pallas as pl
from jax.experimental.pallas import tpu as pltpu
from jax.sharding import PartitionSpec as P

sharpness = 1.5
LANES = 128
F32 = jnp.float32
BF16 = jnp.bfloat16
VMEM = pl.BlockSpec(memory_space=pltpu.VMEM)
PARAMS = pltpu.CompilerParams(vmem_limit_bytes=40 * 1024 * 1024)


def unit_rows(matrix):
    values = matrix.astype(F32)
    return (values * lax.rsqrt(jnp.sum(values * values, axis=1, keepdims=True) + 1e-06)).astype(
        BF16
    )


def plain_body(plan, source, target, source_mass, target_mass):
    sources_unit = unit_rows(lax.all_gather(source, "cols", axis=1, tiled=True))
    targets_unit = unit_rows(lax.all_gather(target, "rows", axis=1, tiled=True))
    projected = jnp.dot(plan, targets_unit, preferred_element_type=F32).astype(BF16)
    partial_coupling = lax.dot_general(
        sources_unit, projected, (((0,), (0,)), ((), ())), preferred_element_type=F32
    )
    coupling = lax.psum(partial_coupling, ("rows", "cols"))
    normalized = (coupling * lax.rsqrt(jnp.sum(coupling * coupling) / 2048.0 + 1e-06)).astype(BF16)
    lifted = jnp.dot(sources_unit, normalized, preferred_element_type=F32).astype(BF16)
    scores = lax.dot_general(
        lifted, targets_unit, (((1,), (1,)), ((), ())), preferred_element_type=F32
    )
    kernel = jnp.exp(sharpness * scores)
    source_count = plan.shape[0] * lax.axis_size("rows")
    target_count = plan.shape[1] * lax.axis_size("cols")
    col_scaling = jnp.ones((plan.shape[1],), F32)
    row_scaling = source_mass
    for repeat in range(2):
        row_totals = lax.psum(jnp.dot(kernel, col_scaling, precision=lax.Precision.HIGHEST), "cols")
        row_scaling = source_mass / (row_totals / target_count)
        col_totals = lax.psum(jnp.dot(row_scaling, kernel, precision=lax.Precision.HIGHEST), "rows")
        col_scaling = target_mass / (col_totals / source_count)
    return (row_scaling, col_scaling)


def kernel_block(targets, near, far, xs_nn, xs_fn, xs_nf, xs_ff, out, sums):
    a, b = near[...], far[...]
    squares = jnp.sum(a.astype(F32) ** 2) + jnp.sum(b.astype(F32) ** 2)
    scale = lax.rsqrt(squares / 2048.0 + 1e-06)
    nt = (((1,), (1,)), ((), ()))
    left_a = (lax.dot_general(targets[...], a, nt, preferred_element_type=F32) * scale).astype(BF16)
    left_b = (lax.dot_general(targets[...], b, nt, preferred_element_type=F32) * scale).astype(BF16)
    width = min(512, xs_nn.shape[1])
    for side, (first, second) in enumerate(((xs_nn, xs_fn), (xs_nf, xs_ff))):

        def step(i, _):
            here = pl.multiple_of(i * width, width)
            scores = jnp.dot(left_a, first[:, pl.ds(here, width)], preferred_element_type=F32)
            scores += jnp.dot(left_b, second[:, pl.ds(here, width)], preferred_element_type=F32)
            block = jnp.exp(sharpness * scores)
            at = pl.multiple_of(side * first.shape[1] + i * width, width)
            out[:, pl.ds(at, width)] = block
            total = jnp.sum(block, axis=0, keepdims=True)
            row = side * (first.shape[1] // LANES) + i * (width // LANES)
            for j in range(width // LANES):
                sums[pl.ds(row + j, 1), :] = total[:, j * LANES : (j + 1) * LANES]
            return 0

        lax.fori_loop(0, xs_nn.shape[1] // width, step, 0)


def weighted(block, base, height, rows):
    total = jnp.zeros((height, LANES), F32)
    for j in range(rows.shape[0]):
        total += block[pl.ds(base, height), j * LANES : (j + 1) * LANES] * rows[j : j + 1, :]
    return total


def sweep(target_count, block, totals, mass, target_mass, sums, acc, rows_ref):
    count, height = block.shape[1], 64
    rows_ref[...] = mass[...] / (totals[...] / target_count)
    acc[...] = jnp.zeros_like(acc)

    def step(i, _):
        base = pl.multiple_of(i * height, height)
        total = jnp.sum(weighted(block, base, height, rows_ref), axis=1, keepdims=True)
        col = target_mass[pl.ds(base, height), :] / (total / count)
        spread = jnp.broadcast_to(col, (height, LANES))
        for j in range(count // LANES):
            part = block[pl.ds(base, height), j * LANES : (j + 1) * LANES] * spread
            acc[j] += jnp.sum(part.reshape(height // 8, 8, LANES), axis=0)
        return 0

    lax.fori_loop(0, block.shape[0] // height, step, 0)
    sums[...] = jnp.sum(acc[...], axis=1)


def last_sweep(target_count, block, totals, mass, target_mass, rows_out, cols_out, rows_ref, acc):
    count, height = block.shape[1], 64
    rows_ref[...] = mass[...] / (totals[...] / target_count)
    rows_out[...] = rows_ref[: rows_out.shape[0], :]

    def step(i, _):
        base = pl.multiple_of(i * height, height)
        acc[pl.ds(base, height), :] = weighted(block, base, height, rows_ref)
        return 0

    lax.fori_loop(0, block.shape[0] // height, step, 0)
    total = jnp.sum(acc[...].T, axis=0, keepdims=True)
    cols_out[...] = target_mass[...] / (total / count)


def body(plan, source, target, source_mass, target_mass):
    n = lax.axis_size("cols")
    outer = n // 4

    def swap(value, bits):
        return lax.ppermute(value, "cols", [(i, i ^ bits) for i in range(n)])

    def cross(value):
        return lax.ppermute(value, "rows", [(0, 1), (1, 0)])

    sources, targets = plan.shape
    target_count = targets * n
    mine = source.T
    pieces = [mine] + [swap(mine, 4 * j) for j in range(1, outer)]
    near = jnp.concatenate(pieces, axis=0)
    near = jnp.concatenate([near, swap(near, 2)], axis=0)

    targets_unit = unit_rows(jnp.concatenate([target, cross(target)], axis=1))
    projected = jnp.dot(plan, targets_unit, preferred_element_type=F32).astype(BF16)
    projected = (projected.astype(F32) + swap(projected, 1).astype(F32)).astype(BF16)

    squares = jnp.sum(near.astype(F32) ** 2, axis=0, keepdims=True)
    inverse = lax.rsqrt(squares + swap(squares, 1) + 1e-06)
    xs_nn = (near.astype(F32) * inverse).astype(BF16)
    xs_nf = cross(xs_nn)
    xs_fn = swap(xs_nn, 1)

    coupling = jnp.dot(xs_nn, projected, preferred_element_type=F32)
    half = coupling.shape[0] // 2
    coupling = coupling[:half] + swap(coupling[half:].astype(BF16), 2).astype(F32)
    step = 1
    while step < outer:
        other = swap(coupling.astype(BF16), 4 * step).astype(F32)
        other = other.reshape(outer // step, step, -1, coupling.shape[1])
        other = jnp.stack([other[i ^ 1] for i in range(outer // step)])
        coupling = coupling + other.reshape(coupling.shape)
        step *= 2
    other = cross(coupling.astype(BF16)).astype(F32)
    split = coupling.shape[1] // 2
    coupling = coupling + jnp.concatenate([other[:, split:], other[:, :split]], axis=1)
    coupling = coupling.astype(BF16)
    coupling = jnp.concatenate([coupling, swap(coupling, 2)], axis=0)
    coupling_far = swap(coupling, 1)
    xs_ff = swap(xs_nf, 1)

    count = 2 * sources
    block, sums = pl.pallas_call(
        kernel_block,
        out_shape=(
            jax.ShapeDtypeStruct((targets, count), F32),
            jax.ShapeDtypeStruct((count // LANES, LANES), F32),
        ),
        in_specs=[VMEM] * 7,
        out_specs=(VMEM, VMEM),
        compiler_params=PARAMS,
    )(targets_unit, coupling, coupling_far, xs_nn, xs_fn, xs_nf, xs_ff)

    def summed(value):
        bits = 1
        while bits < n:
            value = value + swap(value, bits)
            bits *= 2
        return value

    mass = source_mass.reshape(-1, LANES)
    mass = jnp.concatenate([mass, cross(mass)], axis=0)
    rows_scratch = pltpu.VMEM((count // LANES, LANES), F32)
    sums = pl.pallas_call(
        functools.partial(sweep, target_count),
        out_shape=jax.ShapeDtypeStruct((count // LANES, LANES), F32),
        in_specs=[VMEM] * 4,
        out_specs=VMEM,
        scratch_shapes=[pltpu.VMEM((count // LANES, 8, LANES), F32), rows_scratch],
        compiler_params=PARAMS,
    )(block, summed(sums), mass, target_mass.reshape(-1, 1))
    row_scaling, col_scaling = pl.pallas_call(
        functools.partial(last_sweep, target_count),
        out_shape=(
            jax.ShapeDtypeStruct((sources // LANES, LANES), F32),
            jax.ShapeDtypeStruct((1, targets), F32),
        ),
        in_specs=[VMEM] * 4,
        out_specs=(VMEM, VMEM),
        scratch_shapes=[rows_scratch, pltpu.VMEM((targets, LANES), F32)],
        compiler_params=PARAMS,
    )(block, summed(sums), mass, target_mass.reshape(1, -1))
    return (row_scaling.reshape(-1), col_scaling.reshape(-1))


def pick(mesh, plan, source):
    rows, n = mesh.shape["rows"], mesh.shape["cols"]
    features = source[1] // n
    fits = plan[0] * (plan[1] // n) * 4 <= 16 * 1024 * 1024
    even = n >= 8 and n & (n - 1) == 0 and features % 16 == 0
    whole = plan[0] % (rows * 512) == 0 and plan[1] % (n * 128) == 0
    return body if rows == 2 and fits and even and whole else plain_body


def solution(mesh):
    def run(plan, source, target, source_mass, target_mass):
        chosen = pick(mesh, plan.shape, source.shape)
        return jax.shard_map(
            chosen,
            mesh=mesh,
            in_specs=(P("rows", "cols"), P("rows", "cols"), P("cols", "rows"), P("rows"), P("cols")),
            out_specs=(P("rows"), P("cols")),
            check_vma=False,
        )(plan, source, target, source_mass, target_mass)

    return run
```

```python
import functools

import jax
import jax.numpy as jnp
from jax import lax
from jax.experimental import pallas as pl
from jax.experimental.pallas import tpu as pltpu
from jax.sharding import PartitionSpec as P

sharpness = 1.5
LANES = 128
F32 = jnp.float32
BF16 = jnp.bfloat16
VMEM = pl.BlockSpec(memory_space=pltpu.VMEM)
ANY = pl.BlockSpec(memory_space=pl.ANY)
MIB = 1024 * 1024
LOG2E = 1.4426950408889634


def unit_rows(matrix):
    values = matrix.astype(F32)
    return (values * lax.rsqrt(jnp.sum(values * values, axis=1, keepdims=True) + 1e-06)).astype(
        BF16
    )


def plain_body(plan, source, target, source_mass, target_mass):
    sources_unit = unit_rows(lax.all_gather(source, "cols", axis=1, tiled=True))
    targets_unit = unit_rows(lax.all_gather(target, "rows", axis=1, tiled=True))
    projected = jnp.dot(plan, targets_unit, preferred_element_type=F32).astype(BF16)
    partial_coupling = lax.dot_general(
        sources_unit, projected, (((0,), (0,)), ((), ())), preferred_element_type=F32
    )
    coupling = lax.psum(partial_coupling, ("rows", "cols"))
    normalized = (coupling * lax.rsqrt(jnp.sum(coupling * coupling) / 2048.0 + 1e-06)).astype(BF16)
    lifted = jnp.dot(sources_unit, normalized, preferred_element_type=F32).astype(BF16)
    scores = lax.dot_general(
        lifted, targets_unit, (((1,), (1,)), ((), ())), preferred_element_type=F32
    )
    kernel = jnp.exp(sharpness * scores)
    source_count = plan.shape[0] * lax.axis_size("rows")
    target_count = plan.shape[1] * lax.axis_size("cols")
    col_scaling = jnp.ones((plan.shape[1],), F32)
    row_scaling = source_mass
    for repeat in range(2):
        row_totals = lax.psum(jnp.dot(kernel, col_scaling, precision=lax.Precision.HIGHEST), "cols")
        row_scaling = source_mass / (row_totals / target_count)
        col_totals = lax.psum(jnp.dot(row_scaling, kernel, precision=lax.Precision.HIGHEST), "rows")
        col_scaling = target_mass / (col_totals / source_count)
    return (row_scaling, col_scaling)


def unit_targets(plan, near, near_x, units):
    a, b = near[...].astype(F32), near_x[...].astype(F32)
    squares = jnp.sum(a * a, axis=1, keepdims=True) + jnp.sum(b * b, axis=1, keepdims=True)
    inverse = lax.rsqrt(squares + 1e-06)
    units[:, : a.shape[1]] = (a * inverse).astype(BF16)
    units[:, a.shape[1] :] = (b * inverse).astype(BF16)


def project(start, plan, plan_far, units, units_far, out):
    height = min(512, out.shape[0])

    def step(i, _):
        at = pl.multiple_of(i * height, height)
        here = pl.ds(pl.multiple_of(start + i * height, height), height)
        total = jnp.dot(plan[here, :], units[...], preferred_element_type=F32)
        total += jnp.dot(plan_far[here, :], units_far[...], preferred_element_type=F32)
        out[pl.ds(at, height), :] = total.astype(BF16)
        return 0

    lax.fori_loop(0, out.shape[0] // height, step, 0)


def sum_squares(*refs):
    total = 0.0
    for piece in refs[:-1]:
        total += jnp.sum(piece[...].astype(F32) ** 2, axis=0, keepdims=True)
    refs[-1][...] = total


def couple(p0, p1, p2, p3, p4, p5, p6, p7, squares, squares_y, upper, lower, keep, to_x, to_y, to_xy, units):
    inverse = lax.rsqrt(squares[...] + squares_y[...] + 1e-06)
    rows = p0.shape[0]
    for i, piece in enumerate((p0, p1, p2, p3, p4, p5, p6, p7)):
        units[i * rows : (i + 1) * rows, :] = (piece[...].astype(F32) * inverse).astype(BF16)
    half, split = keep.shape
    part = upper.shape[0]
    product = jnp.dot(units[:, :part], upper[...], preferred_element_type=F32)
    product += jnp.dot(units[:, part:], lower[...], preferred_element_type=F32)
    keep[...] = product[:half, :split]
    to_x[...] = product[:half, split:].astype(BF16)
    to_y[...] = product[half:, :split].astype(BF16)
    to_xy[...] = product[half:, split:].astype(BF16)


def kernel_block(targets, c0, x0, c1, x1, c2, x2, c3, x3, near, far, out, sums, left):
    pieces = ((c0, x0), (c1, x1), (c2, x2), (c3, x3))
    rows, split = c0.shape
    squares = 0.0
    for piece in pieces:
        squares += jnp.sum(piece[0][...].astype(F32) ** 2 + piece[1][...].astype(F32) ** 2)
    scale = lax.rsqrt(squares / 2048.0 + 1e-06) * (sharpness * LOG2E)
    nt = (((1,), (1,)), ((), ()))
    for i, piece in enumerate(pieces):
        product = lax.dot_general(targets[:, :split], piece[0][...], nt, preferred_element_type=F32)
        product += lax.dot_general(targets[:, split:], piece[1][...], nt, preferred_element_type=F32)
        left[:, i * rows : (i + 1) * rows] = (product * scale).astype(BF16)
    half = 2 * rows
    width = min(512, near.shape[1])

    def step(i, _):
        here = pl.ds(pl.multiple_of(i * width, width), width)
        scores = jnp.dot(left[:, :half], near[:, here], preferred_element_type=F32)
        scores += jnp.dot(left[:, half:], far[:, here], preferred_element_type=F32)
        block = jnp.exp2(scores)
        out[:, here] = block
        total = jnp.sum(block, axis=0, keepdims=True)
        for j in range(width // LANES):
            row = i * (width // LANES) + j
            sums[pl.ds(row, 1), :] = total[:, j * LANES : (j + 1) * LANES]
        return 0

    lax.fori_loop(0, near.shape[1] // width, step, 0)


def sweep_rows(target_count, block, totals, mass, rows, sums, acc):
    height = 64
    rows[...] = mass[...] / (totals[...] / target_count)

    def step(i, _):
        here = pl.ds(pl.multiple_of(i * height, height), height)
        total = jnp.zeros((height, LANES), F32)
        for j in range(rows.shape[0]):
            total += block[here, j * LANES : (j + 1) * LANES] * rows[j : j + 1, :]
        acc[here, :] = total
        return 0

    lax.fori_loop(0, block.shape[0] // height, step, 0)
    sums[...] = jnp.sum(acc[...].T, axis=0, keepdims=True)


def sweep_cols(source_count, block, totals, totals_x, mass, sums, acc, spread):
    height = 64
    cols = mass[...] / ((totals[...] + totals_x[...]) / source_count)
    spread[...] = jnp.broadcast_to(cols, (LANES, block.shape[0])).T
    acc[...] = jnp.zeros_like(acc)

    def step(i, _):
        here = pl.ds(pl.multiple_of(i * height, height), height)
        for j in range(acc.shape[0]):
            part = block[here, j * LANES : (j + 1) * LANES] * spread[here, :]
            acc[j] += jnp.sum(part.reshape(height // 8, 8, LANES), axis=0)
        return 0

    lax.fori_loop(0, block.shape[0] // height, step, 0)
    sums[...] = jnp.sum(acc[...], axis=1)


def turned(value, order):
    blocks = value.astype(F32).reshape(len(order), -1, value.shape[1])
    return jnp.concatenate([blocks[i] for i in order], axis=0)


def body(plan, source, target, source_mass, target_mass):
    n = lax.axis_size("cols")

    def swap(value, bits):
        return lax.ppermute(value, "cols", [(i, i ^ bits) for i in range(n)])

    def cross(value):
        return lax.ppermute(value, "rows", [(0, 1), (1, 0)])

    def both(value):
        pairs = [(r * n + i, (1 - r) * n + (i ^ 2)) for r in range(2) for i in range(n)]
        return lax.ppermute(value, ("rows", "cols"), pairs)

    def call(function, shapes, *values, scratch=(), mib=16, flops=0, loose=()):
        outs = tuple(jax.ShapeDtypeStruct(shape, kind) for shape, kind in shapes)
        moved = sum(value.size * value.dtype.itemsize for value in values + outs)
        return pl.pallas_call(
            function,
            out_shape=outs,
            in_specs=[ANY if i in loose else VMEM for i in range(len(values))],
            out_specs=(VMEM,) * len(shapes),
            scratch_shapes=[pltpu.VMEM(shape, kind) for shape, kind in scratch],
            compiler_params=pltpu.CompilerParams(vmem_limit_bytes=mib * MIB),
            cost_estimate=pl.CostEstimate(flops=flops, bytes_accessed=moved, transcendentals=0),
        )(*values)

    hold = lax.optimization_barrier
    sources, targets = plan.shape
    target_count = targets * n
    source_count = sources * lax.axis_size("rows")
    features = source.shape[1] * n
    half = features // 4
    split = features // 2

    own = source.T
    z2, z1, y0 = swap(own, 8), swap(own, 4), swap(own, 2)
    wide, part = (targets, features), sources // 2
    target_x = cross(target)
    plan_far = swap(plan, 1)
    (units,) = call(unit_targets, ((wide, BF16),), plan, target, target_x, loose=(0,))
    units, y0, z1, z2 = hold((units, y0, z1, z2))
    units_far = swap(units, 1)
    z3, yz2, yz1 = swap(z2, 4), swap(z2, 2), swap(z1, 2)
    (upper,) = call(
        functools.partial(project, 0),
        (((part, features), BF16),),
        plan,
        plan_far,
        units,
        units_far,
        flops=4 * part * targets * features,
    )
    upper, z3 = hold((upper, z3))
    yz3 = swap(z3, 2)
    (lower,) = call(
        functools.partial(project, part),
        (((part, features), BF16),),
        plan,
        plan_far,
        units,
        units_far,
        flops=4 * part * targets * features,
    )
    (squares,) = call(sum_squares, (((1, sources), F32),), own, z2, z1, z3)
    yz1, yz2, squares, lower = hold((yz1, yz2, squares, lower))
    squares += swap(squares, 1)
    squares_y = swap(squares, 2)
    yz3, squares_y = hold((yz3, squares_y))
    pieces = [own, z2, z1, z3, y0, yz2, yz1, yz3]
    quarter = ((half, split), BF16)
    coupling, to_x, to_y, to_xy, xs = call(
        couple,
        (((half, split), F32), quarter, quarter, quarter, ((split, sources), BF16)),
        *pieces,
        squares,
        squares_y,
        upper,
        lower,
        flops=2 * sources * split * features,
    )
    xs_far = swap(xs, 1)

    for other in (cross(to_x), swap(to_y, 2), both(to_xy)):
        coupling += other.astype(F32)
    coupling += turned(swap(coupling.astype(BF16), 4), (2, 3, 0, 1))
    coupling += turned(swap(coupling.astype(BF16), 8), (1, 0, 3, 2))
    coupling = coupling.astype(BF16)
    blocks = [coupling, cross(coupling), swap(coupling, 2), both(coupling)]
    blocks += [swap(block, 1) for block in blocks]

    tall, wide = (sources // LANES, LANES), (1, targets)
    block, sums = call(
        kernel_block,
        (((targets, sources), F32), (tall, F32)),
        units,
        *blocks,
        xs,
        xs_far,
        scratch=(((targets, features), BF16),),
        flops=2 * targets * features * (sources + features),
    )

    mass, target_mass = source_mass.reshape(tall), target_mass.reshape(wide)
    for repeat in range(2):
        sums = sums + swap(sums, 1)
        sums = sums + swap(sums, 2) + swap(sums, 4) + swap(sums, 6)
        sums = sums + swap(sums, 8)
        rows, totals = call(
            functools.partial(sweep_rows, target_count),
            ((tall, F32), (wide, F32)),
            block,
            sums,
            mass,
            scratch=(((targets, LANES), F32),),
        )
        totals_x = cross(totals)
        if repeat == 0:
            (sums,) = call(
                functools.partial(sweep_cols, source_count),
                ((tall, F32),),
                block,
                totals,
                totals_x,
                target_mass,
                scratch=(((tall[0], 8, LANES), F32), ((targets, LANES), F32)),
            )
    cols = target_mass / ((totals + totals_x) / source_count)
    return (rows.reshape(-1), cols.reshape(-1))


def pick(mesh, plan, source):
    rows, n = mesh.shape["rows"], mesh.shape["cols"]
    features = source[1] // n
    fits = (plan[0] // rows) * (plan[1] // n) * 4 <= 4 * MIB
    even = n == 16 and features % 16 == 0
    whole = plan[0] % (rows * 512) == 0 and plan[1] % (n * 128) == 0
    return body if rows == 2 and fits and even and whole else plain_body


def solution(mesh):
    def run(plan, source, target, source_mass, target_mass):
        chosen = pick(mesh, plan.shape, source.shape)
        return jax.shard_map(
            chosen,
            mesh=mesh,
            in_specs=(P("rows", "cols"), P("rows", "cols"), P("cols", "rows"), P("rows"), P("cols")),
            out_specs=(P("rows"), P("cols")),
            check_vma=False,
        )(plan, source, target, source_mass, target_mass)

    return run
```

```python
import functools

import jax
import jax.numpy as jnp
from jax import lax
from jax.experimental import pallas as pl
from jax.experimental.pallas import tpu as pltpu
from jax.sharding import PartitionSpec as P

sharpness = 1.5
LANES = 128
F32 = jnp.float32
BF16 = jnp.bfloat16
VMEM = pl.BlockSpec(memory_space=pltpu.VMEM)
ANY = pl.BlockSpec(memory_space=pl.ANY)
MIB = 1024 * 1024
LOG2E = 1.4426950408889634


def unit_rows(matrix):
    values = matrix.astype(F32)
    return (values * lax.rsqrt(jnp.sum(values * values, axis=1, keepdims=True) + 1e-06)).astype(
        BF16
    )


def plain_body(plan, source, target, source_mass, target_mass):
    sources_unit = unit_rows(lax.all_gather(source, "cols", axis=1, tiled=True))
    targets_unit = unit_rows(lax.all_gather(target, "rows", axis=1, tiled=True))
    projected = jnp.dot(plan, targets_unit, preferred_element_type=F32).astype(BF16)
    partial_coupling = lax.dot_general(
        sources_unit, projected, (((0,), (0,)), ((), ())), preferred_element_type=F32
    )
    coupling = lax.psum(partial_coupling, ("rows", "cols"))
    normalized = (coupling * lax.rsqrt(jnp.sum(coupling * coupling) / 2048.0 + 1e-06)).astype(BF16)
    lifted = jnp.dot(sources_unit, normalized, preferred_element_type=F32).astype(BF16)
    scores = lax.dot_general(
        lifted, targets_unit, (((1,), (1,)), ((), ())), preferred_element_type=F32
    )
    kernel = jnp.exp(sharpness * scores)
    source_count = plan.shape[0] * lax.axis_size("rows")
    target_count = plan.shape[1] * lax.axis_size("cols")
    col_scaling = jnp.ones((plan.shape[1],), F32)
    row_scaling = source_mass
    for repeat in range(2):
        row_totals = lax.psum(jnp.dot(kernel, col_scaling, precision=lax.Precision.HIGHEST), "cols")
        row_scaling = source_mass / (row_totals / target_count)
        col_totals = lax.psum(jnp.dot(row_scaling, kernel, precision=lax.Precision.HIGHEST), "rows")
        col_scaling = target_mass / (col_totals / source_count)
    return (row_scaling, col_scaling)


def square_targets(plan, near, mass, target_mass, squares, mass_out, target_mass_out):
    mass_out[...] = mass[...]
    target_mass_out[...] = target_mass[...]
    values = near[...].astype(F32)
    total = jnp.sum(values * values, axis=1, keepdims=True)
    squares[...] = jnp.broadcast_to(total, squares.shape)


def unit_targets(near, near_x, squares, units):
    a, b = near[...].astype(F32), near_x[...].astype(F32)
    inverse = lax.rsqrt(squares[:, :1] + jnp.sum(b * b, axis=1, keepdims=True) + 1e-06)
    units[:, : a.shape[1]] = (a * inverse).astype(BF16)
    units[:, a.shape[1] :] = (b * inverse).astype(BF16)


def project(start, plan, plan_far, units, units_far, out):
    height = min(512, out.shape[0])

    def step(i, _):
        at = pl.multiple_of(i * height, height)
        here = pl.ds(pl.multiple_of(start + i * height, height), height)
        total = jnp.dot(plan[here, :], units[...], preferred_element_type=F32)
        total += jnp.dot(plan_far[here, :], units_far[...], preferred_element_type=F32)
        out[pl.ds(at, height), :] = total.astype(BF16)
        return 0

    lax.fori_loop(0, out.shape[0] // height, step, 0)


def sum_squares(*refs):
    total = 0.0
    for piece in refs[:-1]:
        total += jnp.sum(piece[...].astype(F32) ** 2, axis=0, keepdims=True)
    refs[-1][...] = total


def couple(p0, p1, p2, p3, p4, p5, p6, p7, squares, squares_y, upper, lower, keep, to_x, to_y, to_xy, units):
    inverse = lax.rsqrt(squares[...] + squares_y[...] + 1e-06)
    rows = p0.shape[0]
    for i, piece in enumerate((p0, p1, p2, p3, p4, p5, p6, p7)):
        units[i * rows : (i + 1) * rows, :] = (piece[...].astype(F32) * inverse).astype(BF16)
    half, split = keep.shape
    part = upper.shape[0]
    product = jnp.dot(units[:, :part], upper[...], preferred_element_type=F32)
    product += jnp.dot(units[:, part:], lower[...], preferred_element_type=F32)
    keep[...] = product[:half, :split]
    to_x[...] = product[:half, split:].astype(BF16)
    to_y[...] = product[half:, :split].astype(BF16)
    to_xy[...] = product[half:, split:].astype(BF16)


def kernel_block(targets, c0, x0, c1, x1, c2, x2, c3, x3, near, far, out, sums, left, whole):
    rows, split = c0.shape
    for i, pair in enumerate(((c0, x0), (c1, x1), (c2, x2), (c3, x3))):
        for j, piece in enumerate(pair):
            whole[i * rows : (i + 1) * rows, j * split : (j + 1) * split] = piece[...]
    nt = (((1,), (1,)), ((), ()))
    product = lax.dot_general(targets[...], whole[...], nt, preferred_element_type=F32)
    squares = jnp.sum(whole[...].astype(F32) ** 2)
    scale = lax.rsqrt(squares / 2048.0 + 1e-06) * (sharpness * LOG2E)
    left[...] = (product * scale).astype(BF16)
    half = 2 * rows
    width = min(512, near.shape[1])
    for start in range(0, near.shape[1], width):
        here = slice(start, start + width)
        scores = jnp.dot(left[:, :half], near[:, here], preferred_element_type=F32)
        scores += jnp.dot(left[:, half:], far[:, here], preferred_element_type=F32)
        block = jnp.exp2(scores)
        out[:, here] = block
        total = jnp.sum(block, axis=0, keepdims=True)
        for j in range(width // LANES):
            row = start // LANES + j
            sums[row : row + 1, :] = total[:, j * LANES : (j + 1) * LANES]


def sweep_rows(target_count, block, totals, mass, sums, rows, acc):
    rows[...] = mass[...] / (totals[...] / target_count)
    for start in range(0, block.shape[0], 64):
        here = slice(start, start + 64)
        total = jnp.zeros((64, LANES), F32)
        for j in range(rows.shape[0]):
            total += block[here, j * LANES : (j + 1) * LANES] * rows[j : j + 1, :]
        acc[here, :] = total
    sums[...] = jnp.sum(acc[...].T, axis=0, keepdims=True)


def sweep_cols(source_count, block, totals, totals_x, mass, sums, acc, spread):
    cols = mass[...] / ((totals[...] + totals_x[...]) / source_count)
    spread[...] = jnp.broadcast_to(cols, (LANES, block.shape[0])).T
    acc[...] = jnp.zeros_like(acc)
    for start in range(0, block.shape[0], 64):
        here = slice(start, start + 64)
        for j in range(acc.shape[0]):
            part = block[here, j * LANES : (j + 1) * LANES] * spread[here, :]
            acc[j] += jnp.sum(part.reshape(8, 8, LANES), axis=0)
    sums[...] = jnp.sum(acc[...], axis=1)


def finish(source_count, rows_in, totals, totals_x, mass, rows, cols):
    rows[...] = rows_in[...]
    cols[...] = mass[...] / ((totals[...] + totals_x[...]) / source_count)


def turned(value, order):
    blocks = value.astype(F32).reshape(len(order), -1, value.shape[1])
    return jnp.concatenate([blocks[i] for i in order], axis=0)


def body(plan, source, target, source_mass, target_mass):
    n = lax.axis_size("cols")

    def swap(value, bits):
        return lax.ppermute(value, "cols", [(i, i ^ bits) for i in range(n)])

    def cross(value):
        return lax.ppermute(value, "rows", [(0, 1), (1, 0)])

    def both(value):
        pairs = [(r * n + i, (1 - r) * n + (i ^ 3)) for r in range(2) for i in range(n)]
        return lax.ppermute(value, ("rows", "cols"), pairs)

    def call(function, shapes, *values, scratch=(), mib=16, flops=0, loose=()):
        outs = tuple(jax.ShapeDtypeStruct(shape, kind) for shape, kind in shapes)
        moved = sum(value.size * value.dtype.itemsize for value in values + outs)
        return pl.pallas_call(
            function,
            out_shape=outs,
            in_specs=[ANY if i in loose else VMEM for i in range(len(values))],
            out_specs=(VMEM,) * len(shapes),
            scratch_shapes=[pltpu.VMEM(shape, kind) for shape, kind in scratch],
            compiler_params=pltpu.CompilerParams(vmem_limit_bytes=mib * MIB),
            cost_estimate=pl.CostEstimate(flops=flops, bytes_accessed=moved, transcendentals=0),
        )(*values)

    hold = lax.optimization_barrier
    sources, targets = plan.shape
    target_count = targets * n
    source_count = sources * lax.axis_size("rows")
    features = source.shape[1] * n
    half = features // 4
    split = features // 2

    own = source.T
    z2, z1, y0 = swap(own, 9), swap(own, 5), swap(own, 3)
    wide, part = (targets, features), sources // 2
    target_x = cross(target)
    plan_far = swap(plan, 1)
    tall, flat = (sources // LANES, LANES), (1, targets)
    weights, mass, target_mass = call(
        square_targets,
        (((targets, LANES), F32), (tall, F32), (flat, F32)),
        plan,
        target,
        source_mass.reshape(tall),
        target_mass.reshape(flat),
        loose=(0,),
    )
    weights, y0, z1, z2 = hold((weights, y0, z1, z2))
    z3, yz2, yz1 = swap(z2, 5), swap(z2, 3), swap(z1, 3)
    target_x, z1 = hold((target_x, z1))
    (units,) = call(unit_targets, ((wide, BF16),), target, target_x, weights)
    units_far = swap(units, 1)
    (upper,) = call(
        functools.partial(project, 0),
        (((part, features), BF16),),
        plan,
        plan_far,
        units,
        units_far,
        flops=4 * part * targets * features,
    )
    upper, yz1, z3 = hold((upper, yz1, z3))
    yz3 = swap(z3, 3)
    (lower,) = call(
        functools.partial(project, part),
        (((part, features), BF16),),
        plan,
        plan_far,
        units,
        units_far,
        flops=4 * part * targets * features,
    )
    (squares,) = call(sum_squares, (((1, sources), F32),), own, z2, z1, z3)

    squares += swap(squares, 1)
    yz2, squares = hold((yz2, squares))
    squares_y = swap(squares, 3)
    yz3, squares_y, lower = hold((yz3, squares_y, lower))
    pieces = [own, z2, z1, z3, y0, yz2, yz1, yz3]
    quarter = ((half, split), BF16)
    coupling, to_x, to_y, to_xy, xs = call(
        couple,
        (((half, split), F32), quarter, quarter, quarter, ((split, sources), BF16)),
        *pieces,
        squares,
        squares_y,
        upper,
        lower,
        flops=2 * sources * split * features,
    )
    xs_far = swap(xs, 1)

    for other in (cross(to_x), swap(to_y, 3), both(to_xy)):
        coupling += other.astype(F32)
    coupling += turned(swap(coupling.astype(BF16), 5), (2, 3, 0, 1))
    coupling += turned(swap(coupling.astype(BF16), 9), (1, 0, 3, 2))
    coupling = coupling.astype(BF16)
    blocks = [coupling, cross(coupling), swap(coupling, 3), both(coupling)]
    blocks += [swap(block, 1) for block in blocks]

    block, sums = call(
        kernel_block,
        (((targets, sources), F32), (tall, F32)),
        units,
        *blocks,
        xs,
        xs_far,
        scratch=(((targets, features), BF16), ((features, features), BF16)),
        flops=2 * targets * features * (sources + features),
    )

    for repeat in range(2):
        sums = sums + swap(sums, 1)
        sums = sums + swap(sums, 3) + swap(sums, 5) + swap(sums, 7)
        sums = sums + swap(sums, 9)
        shapes, scratch = ((flat, F32), (tall, F32)), (((targets, LANES), F32),)
        totals, *rows = call(
            functools.partial(sweep_rows, target_count),
            shapes[: 1 + repeat],
            block,
            sums,
            mass,
            scratch=scratch if repeat else shapes[1:] + scratch,
        )
        totals_x = cross(totals)
        if repeat == 0:
            (sums,) = call(
                functools.partial(sweep_cols, source_count),
                ((tall, F32),),
                block,
                totals,
                totals_x,
                target_mass,
                scratch=(((tall[0], 8, LANES), F32), ((targets, LANES), F32)),
            )
    rows, cols = call(
        functools.partial(finish, source_count),
        ((tall, F32), (flat, F32)),
        rows[0],
        totals,
        totals_x,
        target_mass,
    )
    return (rows.reshape(-1), cols.reshape(-1))


def pick(mesh, plan, source):
    rows, n = mesh.shape["rows"], mesh.shape["cols"]
    features = source[1] // n
    fits = (plan[0] // rows) * (plan[1] // n) * 4 <= 4 * MIB
    even = n == 16 and features % 16 == 0
    whole = plan[0] % (rows * 512) == 0 and plan[1] % (n * 128) == 0
    return body if rows == 2 and fits and even and whole else plain_body


def solution(mesh):
    def run(plan, source, target, source_mass, target_mass):
        chosen = pick(mesh, plan.shape, source.shape)
        return jax.shard_map(
            chosen,
            mesh=mesh,
            in_specs=(P("rows", "cols"), P("rows", "cols"), P("cols", "rows"), P("rows"), P("cols")),
            out_specs=(P("rows"), P("cols")),
            check_vma=False,
        )(plan, source, target, source_mass, target_mass)

    return run
```

```python
import functools

import jax
import jax.numpy as jnp
from jax import lax
from jax.experimental import pallas as pl
from jax.experimental.pallas import tpu as pltpu
from jax.sharding import PartitionSpec as P

sharpness = 1.5
LANES = 128
F32 = jnp.float32
BF16 = jnp.bfloat16
VMEM = pl.BlockSpec(memory_space=pltpu.VMEM)
ANY = pl.BlockSpec(memory_space=pl.ANY)
MIB = 1024 * 1024
LOG2E = 1.4426950408889634


def unit_rows(matrix):
    values = matrix.astype(F32)
    return (values * lax.rsqrt(jnp.sum(values * values, axis=1, keepdims=True) + 1e-06)).astype(
        BF16
    )


def plain_body(plan, source, target, source_mass, target_mass):
    sources_unit = unit_rows(lax.all_gather(source, "cols", axis=1, tiled=True))
    targets_unit = unit_rows(lax.all_gather(target, "rows", axis=1, tiled=True))
    projected = jnp.dot(plan, targets_unit, preferred_element_type=F32).astype(BF16)
    partial_coupling = lax.dot_general(
        sources_unit, projected, (((0,), (0,)), ((), ())), preferred_element_type=F32
    )
    coupling = lax.psum(partial_coupling, ("rows", "cols"))
    normalized = (coupling * lax.rsqrt(jnp.sum(coupling * coupling) / 2048.0 + 1e-06)).astype(BF16)
    lifted = jnp.dot(sources_unit, normalized, preferred_element_type=F32).astype(BF16)
    scores = lax.dot_general(
        lifted, targets_unit, (((1,), (1,)), ((), ())), preferred_element_type=F32
    )
    kernel = jnp.exp(sharpness * scores)
    source_count = plan.shape[0] * lax.axis_size("rows")
    target_count = plan.shape[1] * lax.axis_size("cols")
    col_scaling = jnp.ones((plan.shape[1],), F32)
    row_scaling = source_mass
    for repeat in range(2):
        row_totals = lax.psum(jnp.dot(kernel, col_scaling, precision=lax.Precision.HIGHEST), "cols")
        row_scaling = source_mass / (row_totals / target_count)
        col_totals = lax.psum(jnp.dot(row_scaling, kernel, precision=lax.Precision.HIGHEST), "rows")
        col_scaling = target_mass / (col_totals / source_count)
    return (row_scaling, col_scaling)


def square_targets(plan, near, mass, target_mass, squares, mass_out, target_mass_out):
    mass_out[...] = mass[...]
    target_mass_out[...] = target_mass[...]
    values = near[...].astype(F32)
    total = jnp.sum(values * values, axis=1, keepdims=True)
    squares[...] = jnp.broadcast_to(total, squares.shape)


def unit_targets(near, near_x, squares, units):
    a, b = near[...].astype(F32), near_x[...].astype(F32)
    inverse = lax.rsqrt(squares[:, :1] + jnp.sum(b * b, axis=1, keepdims=True) + 1e-06)
    units[:, : a.shape[1]] = (a * inverse).astype(BF16)
    units[:, a.shape[1] :] = (b * inverse).astype(BF16)


def project(start, plan, plan_far, units, units_far, out):
    height = min(512, out.shape[0])

    def step(i, _):
        at = pl.multiple_of(i * height, height)
        here = pl.ds(pl.multiple_of(start + i * height, height), height)
        total = jnp.dot(plan[here, :], units[...], preferred_element_type=F32)
        total += jnp.dot(plan_far[here, :], units_far[...], preferred_element_type=F32)
        out[pl.ds(at, height), :] = total.astype(BF16)
        return 0

    lax.fori_loop(0, out.shape[0] // height, step, 0)


def sum_squares(*refs):
    total = 0.0
    for piece in refs[:-1]:
        total += jnp.sum(piece[...].astype(F32) ** 2, axis=0, keepdims=True)
    refs[-1][...] = total


def couple(p0, p1, p2, p3, p4, p5, p6, p7, squares, squares_y, upper, lower, keep, to_x, to_y, to_xy, units):
    inverse = lax.rsqrt(squares[...] + squares_y[...] + 1e-06)
    rows = p0.shape[0]
    for i, piece in enumerate((p0, p1, p2, p3, p4, p5, p6, p7)):
        units[i * rows : (i + 1) * rows, :] = (piece[...].astype(F32) * inverse).astype(BF16)
    half, split = keep.shape
    part = upper.shape[0]
    product = jnp.dot(units[:, :part], upper[...], preferred_element_type=F32)
    product += jnp.dot(units[:, part:], lower[...], preferred_element_type=F32)
    keep[...] = product[:half, :split]
    to_x[...] = product[:half, split:].astype(BF16)
    to_y[...] = product[half:, :split].astype(BF16)
    to_xy[...] = product[half:, split:].astype(BF16)


def kernel_block(targets, c0, x0, c1, x1, c2, x2, c3, x3, near, far, out, sums, left, whole):
    rows, split = c0.shape
    for i, pair in enumerate(((c0, x0), (c1, x1), (c2, x2), (c3, x3))):
        for j, piece in enumerate(pair):
            whole[i * rows : (i + 1) * rows, j * split : (j + 1) * split] = piece[...]
    nt = (((1,), (1,)), ((), ()))
    product = lax.dot_general(targets[...], whole[...], nt, preferred_element_type=F32)
    squares = jnp.sum(whole[...].astype(F32) ** 2)
    scale = lax.rsqrt(squares / 2048.0 + 1e-06) * (sharpness * LOG2E)
    left[...] = (product * scale).astype(BF16)
    half = 2 * rows
    width = min(512, near.shape[1])
    for start in range(0, near.shape[1], width):
        here = slice(start, start + width)
        scores = jnp.dot(left[:, :half], near[:, here], preferred_element_type=F32)
        scores += jnp.dot(left[:, half:], far[:, here], preferred_element_type=F32)
        block = jnp.exp2(scores)
        out[:, here] = block
        total = jnp.sum(block, axis=0, keepdims=True)
        for j in range(width // LANES):
            row = start // LANES + j
            sums[row : row + 1, :] = total[:, j * LANES : (j + 1) * LANES]


def sweep_rows(target_count, block, totals, mass, sums, rows, acc):
    rows[...] = mass[...] / (totals[...] / target_count)
    for start in range(0, block.shape[0], 64):
        here = slice(start, start + 64)
        total = jnp.zeros((64, LANES), F32)
        for j in range(rows.shape[0]):
            total += block[here, j * LANES : (j + 1) * LANES] * rows[j : j + 1, :]
        acc[here, :] = total
    sums[...] = jnp.sum(acc[...].T, axis=0, keepdims=True)


def sweep_cols(source_count, block, totals, totals_x, mass, sums, acc, spread):
    cols = mass[...] / ((totals[...] + totals_x[...]) / source_count)
    spread[...] = jnp.broadcast_to(cols, (LANES, block.shape[0])).T
    acc[...] = jnp.zeros_like(acc)
    for start in range(0, block.shape[0], 64):
        here = slice(start, start + 64)
        for j in range(acc.shape[0]):
            part = block[here, j * LANES : (j + 1) * LANES] * spread[here, :]
            acc[j] += jnp.sum(part.reshape(8, 8, LANES), axis=0)
    sums[...] = jnp.sum(acc[...], axis=1)


def finish(source_count, rows_in, totals, totals_x, mass, rows, cols):
    rows[...] = rows_in[...]
    cols[...] = mass[...] / ((totals[...] + totals_x[...]) / source_count)


def turned(value, order):
    blocks = value.astype(F32).reshape(len(order), -1, value.shape[1])
    return jnp.concatenate([blocks[i] for i in order], axis=0)


def body(plan, source, target, source_mass, target_mass):
    n = lax.axis_size("cols")

    def swap(value, bits):
        return lax.ppermute(value, "cols", [(i, i ^ bits) for i in range(n)])

    def cross(value):
        return lax.ppermute(value, "rows", [(0, 1), (1, 0)])

    def both(value):
        pairs = [(r * n + i, (1 - r) * n + (i ^ 3)) for r in range(2) for i in range(n)]
        return lax.ppermute(value, ("rows", "cols"), pairs)

    def call(function, shapes, *values, scratch=(), mib=16, flops=0, loose=()):
        outs = tuple(jax.ShapeDtypeStruct(shape, kind) for shape, kind in shapes)
        moved = sum(value.size * value.dtype.itemsize for value in values + outs)
        return pl.pallas_call(
            function,
            out_shape=outs,
            in_specs=[ANY if i in loose else VMEM for i in range(len(values))],
            out_specs=(VMEM,) * len(shapes),
            scratch_shapes=[pltpu.VMEM(shape, kind) for shape, kind in scratch],
            compiler_params=pltpu.CompilerParams(vmem_limit_bytes=mib * MIB),
            cost_estimate=pl.CostEstimate(flops=flops, bytes_accessed=moved, transcendentals=0),
        )(*values)

    hold = lax.optimization_barrier
    sources, targets = plan.shape
    target_count = targets * n
    source_count = sources * lax.axis_size("rows")
    features = source.shape[1] * n
    half = features // 4
    split = features // 2

    own = source.T
    z2, z1, y0 = swap(own, 9), swap(own, 5), swap(own, 3)
    wide, part = (targets, features), sources // 2
    target_x = cross(target)
    plan_far = swap(plan, 1)
    tall, flat = (sources // LANES, LANES), (1, targets)
    weights, mass, target_mass = call(
        square_targets,
        (((targets, LANES), F32), (tall, F32), (flat, F32)),
        plan,
        target,
        source_mass.reshape(tall),
        target_mass.reshape(flat),
        loose=(0,),
    )
    weights, y0, z1, z2 = hold((weights, y0, z1, z2))
    z3, yz2, yz1 = swap(z2, 5), swap(z2, 3), swap(y0, 5)
    target_x, z1 = hold((target_x, z1))
    (units,) = call(unit_targets, ((wide, BF16),), target, target_x, weights)
    units_far = swap(units, 1)
    (upper,) = call(
        functools.partial(project, 0),
        (((part, features), BF16),),
        plan,
        plan_far,
        units,
        units_far,
        flops=4 * part * targets * features,
    )
    upper, z3 = hold((upper, z3))
    yz3 = swap(z3, 3)
    near_units, yz2 = hold((units, yz2))
    (lower,) = call(
        functools.partial(project, part),
        (((part, features), BF16),),
        plan,
        plan_far,
        near_units,
        units_far,
        flops=4 * part * targets * features,
    )
    (squares,) = call(sum_squares, (((1, sources), F32),), own, z2, z1, z3)

    squares += swap(squares, 1)
    squares_y = swap(squares, 3)
    yz3, yz1, squares_y, lower = hold((yz3, yz1, squares_y, lower))
    pieces = [own, z2, z1, z3, y0, yz2, yz1, yz3]
    quarter = ((half, split), BF16)
    coupling, to_x, to_y, to_xy, xs = call(
        couple,
        (((half, split), F32), quarter, quarter, quarter, ((split, sources), BF16)),
        *pieces,
        squares,
        squares_y,
        upper,
        lower,
        flops=2 * sources * split * features,
    )
    xs_far = swap(xs, 1)

    for other in (cross(to_x), swap(to_y, 3), both(to_xy)):
        coupling += other.astype(F32)
    coupling += turned(swap(coupling.astype(BF16), 5), (2, 3, 0, 1))
    coupling += turned(swap(coupling.astype(BF16), 9), (1, 0, 3, 2))
    coupling = coupling.astype(BF16)
    blocks = [coupling, cross(coupling), swap(coupling, 3), both(coupling)]
    blocks += [swap(block, 1) for block in blocks]

    block, sums = call(
        kernel_block,
        (((targets, sources), F32), (tall, F32)),
        units,
        *blocks,
        xs,
        xs_far,
        scratch=(((targets, features), BF16), ((features, features), BF16)),
        flops=2 * targets * features * (sources + features),
    )

    for repeat in range(2):
        sums = sums + swap(sums, 1)
        sums = sums + swap(sums, 3) + swap(sums, 5) + swap(sums, 7)
        sums = sums + swap(sums, 9)
        shapes, scratch = ((flat, F32), (tall, F32)), (((targets, LANES), F32),)
        totals, *rows = call(
            functools.partial(sweep_rows, target_count),
            shapes[: 1 + repeat],
            block,
            sums,
            mass,
            scratch=scratch if repeat else shapes[1:] + scratch,
        )
        totals_x = cross(totals)
        if repeat == 0:
            (sums,) = call(
                functools.partial(sweep_cols, source_count),
                ((tall, F32),),
                block,
                totals,
                totals_x,
                target_mass,
                scratch=(((tall[0], 8, LANES), F32), ((targets, LANES), F32)),
            )
    rows, cols = call(
        functools.partial(finish, source_count),
        ((tall, F32), (flat, F32)),
        rows[0],
        totals,
        totals_x,
        target_mass,
    )
    return (rows.reshape(-1), cols.reshape(-1))


def pick(mesh, plan, source):
    rows, n = mesh.shape["rows"], mesh.shape["cols"]
    features = source[1] // n
    fits = (plan[0] // rows) * (plan[1] // n) * 4 <= 4 * MIB
    even = n == 16 and features % 16 == 0
    whole = plan[0] % (rows * 512) == 0 and plan[1] % (n * 128) == 0
    return body if rows == 2 and fits and even and whole else plain_body


def solution(mesh):
    def run(plan, source, target, source_mass, target_mass):
        chosen = pick(mesh, plan.shape, source.shape)
        return jax.shard_map(
            chosen,
            mesh=mesh,
            in_specs=(P("rows", "cols"), P("rows", "cols"), P("cols", "rows"), P("rows"), P("cols")),
            out_specs=(P("rows"), P("cols")),
            check_vma=False,
        )(plan, source, target, source_mass, target_mass)

    return run
```

```python
import functools

import jax
import jax.numpy as jnp
from jax import lax
from jax.experimental import pallas as pl
from jax.experimental.pallas import tpu as pltpu
from jax.sharding import PartitionSpec as P

sharpness = 1.5
LANES = 128
F32 = jnp.float32
BF16 = jnp.bfloat16
VMEM = pl.BlockSpec(memory_space=pltpu.VMEM)
ANY = pl.BlockSpec(memory_space=pl.ANY)
MIB = 1024 * 1024
LOG2E = 1.4426950408889634


def unit_rows(matrix):
    values = matrix.astype(F32)
    return (values * lax.rsqrt(jnp.sum(values * values, axis=1, keepdims=True) + 1e-06)).astype(
        BF16
    )


def plain_body(plan, source, target, source_mass, target_mass):
    sources_unit = unit_rows(lax.all_gather(source, "cols", axis=1, tiled=True))
    targets_unit = unit_rows(lax.all_gather(target, "rows", axis=1, tiled=True))
    projected = jnp.dot(plan, targets_unit, preferred_element_type=F32).astype(BF16)
    partial_coupling = lax.dot_general(
        sources_unit, projected, (((0,), (0,)), ((), ())), preferred_element_type=F32
    )
    coupling = lax.psum(partial_coupling, ("rows", "cols"))
    normalized = (coupling * lax.rsqrt(jnp.sum(coupling * coupling) / 2048.0 + 1e-06)).astype(BF16)
    lifted = jnp.dot(sources_unit, normalized, preferred_element_type=F32).astype(BF16)
    scores = lax.dot_general(
        lifted, targets_unit, (((1,), (1,)), ((), ())), preferred_element_type=F32
    )
    kernel = jnp.exp(sharpness * scores)
    source_count = plan.shape[0] * lax.axis_size("rows")
    target_count = plan.shape[1] * lax.axis_size("cols")
    col_scaling = jnp.ones((plan.shape[1],), F32)
    row_scaling = source_mass
    for repeat in range(2):
        row_totals = lax.psum(jnp.dot(kernel, col_scaling, precision=lax.Precision.HIGHEST), "cols")
        row_scaling = source_mass / (row_totals / target_count)
        col_totals = lax.psum(jnp.dot(row_scaling, kernel, precision=lax.Precision.HIGHEST), "rows")
        col_scaling = target_mass / (col_totals / source_count)
    return (row_scaling, col_scaling)


def square_targets(plan, near, mass, target_mass, squares, mass_out, target_mass_out):
    mass_out[...] = mass[...]
    target_mass_out[...] = target_mass[...]
    values = near[...].astype(F32)
    total = jnp.sum(values * values, axis=1, keepdims=True)
    squares[...] = jnp.broadcast_to(total, squares.shape)


def half_index():
    index = lax.axis_index("cols")
    return (index ^ (index >> 1) ^ (index >> 2) ^ (index >> 3)) & 1


def unit_targets(near, near_x, squares, units):
    a, b = near[...].astype(F32), near_x[...].astype(F32)
    inverse = lax.rsqrt(squares[:, :1] + jnp.sum(b * b, axis=1, keepdims=True) + 1e-06)
    units[:, : a.shape[1]] = (a * inverse).astype(BF16)
    units[:, a.shape[1] :] = (b * inverse).astype(BF16)


def project(start, plan, plan_far, units, units_far, out):
    height = min(512, out.shape[0])

    def step(i, _):
        at = pl.multiple_of(i * height, height)
        here = pl.ds(pl.multiple_of(start + i * height, height), height)
        total = jnp.dot(plan[here, :], units[...], preferred_element_type=F32)
        total += jnp.dot(plan_far[here, :], units_far[...], preferred_element_type=F32)
        out[pl.ds(at, height), :] = total.astype(BF16)
        return 0

    lax.fori_loop(0, out.shape[0] // height, step, 0)


def sum_squares(*refs):
    total = 0.0
    for piece in refs[:-1]:
        total += jnp.sum(piece[...].astype(F32) ** 2, axis=0, keepdims=True)
    refs[-1][...] = total


def couple(
    p0, p1, p2, p3, p4, p5, p6, p7, squares, squares_y, upper, lower,
    keep, to_x, to_y, to_xy, units,
):
    inverse = lax.rsqrt(squares[...] + squares_y[...] + 1e-06)
    rows = p0.shape[0]
    for i, piece in enumerate((p0, p1, p2, p3, p4, p5, p6, p7)):
        units[i * rows : (i + 1) * rows, :] = (piece[...].astype(F32) * inverse).astype(BF16)
    half, split = keep.shape
    part = upper.shape[0]
    product = jnp.dot(units[:, :part], upper[...], preferred_element_type=F32)
    product += jnp.dot(units[:, part:], lower[...], preferred_element_type=F32)
    keep[...] = product[:half, :split]
    to_x[...] = product[:half, split:].astype(BF16)
    to_y[...] = product[half:, :split].astype(BF16)
    to_xy[...] = product[half:, split:].astype(BF16)


def kernel_block(targets, targets_far, c0, x0, c1, x1, c2, x2, c3, x3, near, far, out, sums, left, whole):
    rows, split = c0.shape
    for i, pair in enumerate(((c0, x0), (c1, x1), (c2, x2), (c3, x3))):
        for j, piece in enumerate(pair):
            whole[i * rows : (i + 1) * rows, j * split : (j + 1) * split] = piece[...]
    nt = (((1,), (1,)), ((), ()))
    squares = jnp.sum(whole[...].astype(F32) ** 2)
    scale = lax.rsqrt(squares / 2048.0 + 1e-06) * (sharpness * LOG2E)
    count = targets.shape[0]
    for i, points in enumerate((targets, targets_far)):
        product = lax.dot_general(points[...], whole[...], nt, preferred_element_type=F32)
        left[i * count : (i + 1) * count, :] = (product * scale).astype(BF16)
    half = 2 * rows
    count = out.shape[1]
    width, first = min(512, count), half_index() * count
    for start in range(0, count, width):
        here = slice(start, start + width)
        there = pl.ds(pl.multiple_of(first + start, width), width)
        scores = jnp.dot(left[:, :half], near[:, there], preferred_element_type=F32)
        scores += jnp.dot(left[:, half:], far[:, there], preferred_element_type=F32)
        block = jnp.exp2(scores)
        out[:, here] = block
        total = jnp.sum(block, axis=0, keepdims=True)
        for j in range(width // LANES):
            row = start // LANES + j
            sums[row : row + 1, :] = total[:, j * LANES : (j + 1) * LANES]


def sweep_rows(target_count, block, totals, mass, sums, rows, acc):
    count = rows.shape[0]
    start = pl.multiple_of(half_index() * count, count)
    rows[...] = mass[pl.ds(start, count), :] / (totals[...] / target_count)
    for start in range(0, block.shape[0], 64):
        here = slice(start, start + 64)
        total = jnp.zeros((64, LANES), F32)
        for j in range(rows.shape[0]):
            total += block[here, j * LANES : (j + 1) * LANES] * rows[j : j + 1, :]
        acc[here, :] = total
    sums[...] = jnp.sum(acc[...].T, axis=0, keepdims=True)


def chip_totals(own, core, both, x):
    count = own.shape[1] // 2
    other = core[...] + both[...]
    other = jnp.concatenate([other[:, count:], other[:, :count]], axis=1)
    return own[...] + x[...] + other


def sweep_cols(source_count, block, own, core, both, x, mass, mass_far, sums, acc, spread):
    masses = jnp.concatenate([mass[...], mass_far[...]], axis=1)
    cols = masses / (chip_totals(own, core, both, x) / source_count)
    spread[...] = jnp.broadcast_to(cols, (LANES, block.shape[0])).T
    acc[...] = jnp.zeros_like(acc)
    for start in range(0, block.shape[0], 64):
        here = slice(start, start + 64)
        for j in range(acc.shape[0]):
            part = block[here, j * LANES : (j + 1) * LANES] * spread[here, :]
            acc[j] += jnp.sum(part.reshape(8, 8, LANES), axis=0)
    sums[...] = jnp.sum(acc[...], axis=1)


def finish(source_count, rows_own, rows_far, own, core, both, x, mass, rows, cols):
    count, mine = rows_own.shape[0], half_index()
    rows[pl.ds(pl.multiple_of(mine * count, count), count), :] = rows_own[...]
    rows[pl.ds(pl.multiple_of((1 - mine) * count, count), count), :] = rows_far[...]
    totals = chip_totals(own, core, both, x)[:, : cols.shape[1]]
    cols[...] = mass[...] / (totals / source_count)


def turned(value, order):
    blocks = value.astype(F32).reshape(len(order), -1, value.shape[1])
    return jnp.concatenate([blocks[i] for i in order], axis=0)


def body(plan, source, target, source_mass, target_mass):
    n = lax.axis_size("cols")

    def swap(value, bits):
        return lax.ppermute(value, "cols", [(i, i ^ bits) for i in range(n)])

    def cross(value):
        return lax.ppermute(value, "rows", [(0, 1), (1, 0)])

    def both(value, bits):
        pairs = [(r * n + i, (1 - r) * n + (i ^ bits)) for r in range(2) for i in range(n)]
        return lax.ppermute(value, ("rows", "cols"), pairs)

    def call(function, shapes, *values, scratch=(), mib=16, flops=0, loose=()):
        outs = tuple(jax.ShapeDtypeStruct(shape, kind) for shape, kind in shapes)
        moved = sum(value.size * value.dtype.itemsize for value in values + outs)
        return pl.pallas_call(
            function,
            out_shape=outs,
            in_specs=[ANY if i in loose else VMEM for i in range(len(values))],
            out_specs=(VMEM,) * len(shapes),
            scratch_shapes=[pltpu.VMEM(shape, kind) for shape, kind in scratch],
            compiler_params=pltpu.CompilerParams(vmem_limit_bytes=mib * MIB),
            cost_estimate=pl.CostEstimate(flops=flops, bytes_accessed=moved, transcendentals=0),
        )(*values)

    hold = lax.optimization_barrier
    sources, targets = plan.shape
    target_count = targets * n
    source_count = sources * lax.axis_size("rows")
    features = source.shape[1] * n
    half = features // 4
    split = features // 2

    own = source.T
    z2, z1, y0 = swap(own, 9), swap(own, 5), swap(own, 3)
    wide, part = (targets, features), sources // 2
    target_x = cross(target)
    plan_far = swap(plan, 1)
    tall, flat = (sources // LANES, LANES), (1, targets)
    weights, mass, target_mass = call(
        square_targets,
        (((targets, LANES), F32), (tall, F32), (flat, F32)),
        plan,
        target,
        source_mass.reshape(tall),
        target_mass.reshape(flat),
        loose=(0,),
    )
    weights, y0, z1, z2 = hold((weights, y0, z1, z2))
    z3, yz2, yz1 = swap(z2, 5), swap(z2, 3), swap(y0, 5)
    target_x, z1 = hold((target_x, z1))
    (units,) = call(unit_targets, ((wide, BF16),), target, target_x, weights)
    units_far = swap(units, 1)
    (upper,) = call(
        functools.partial(project, 0),
        (((part, features), BF16),),
        plan,
        plan_far,
        units,
        units_far,
        flops=4 * part * targets * features,
    )
    target_mass_far = swap(target_mass, 1)
    upper, target_mass_far, z3 = hold((upper, target_mass_far, z3))
    yz3 = swap(z3, 3)
    near_units, yz2 = hold((units, yz2))
    (lower,) = call(
        functools.partial(project, part),
        (((part, features), BF16),),
        plan,
        plan_far,
        near_units,
        units_far,
        flops=4 * part * targets * features,
    )
    (squares,) = call(sum_squares, (((1, sources), F32),), own, z2, z1, z3)

    squares += swap(squares, 1)
    squares_y = swap(squares, 3)
    yz3, yz1, squares_y, lower = hold((yz3, yz1, squares_y, lower))
    pieces = [own, z2, z1, z3, y0, yz2, yz1, yz3]
    quarter = ((half, split), BF16)
    coupling, to_x, to_y, to_xy, xs = call(
        couple,
        (((half, split), F32), quarter, quarter, quarter, ((split, sources), BF16)),
        *pieces,
        squares,
        squares_y,
        upper,
        lower,
        flops=2 * sources * split * features,
    )
    xs_far = swap(xs, 1)

    for other in (cross(to_x), swap(to_y, 3), both(to_xy, 3)):
        coupling += other.astype(F32)
    coupling += turned(swap(coupling.astype(BF16), 5), (2, 3, 0, 1))
    coupling += turned(swap(coupling.astype(BF16), 9), (1, 0, 3, 2))
    coupling = coupling.astype(BF16)
    blocks = [coupling, cross(coupling), swap(coupling, 3), both(coupling, 3)]
    blocks += [swap(block, 1) for block in blocks]

    chip, count = 2 * targets, sources // 2
    part, wide = (count // LANES, LANES), (1, chip)
    block, sums = call(
        kernel_block,
        (((chip, count), F32), (part, F32)),
        units,
        units_far,
        *blocks,
        xs,
        xs_far,
        scratch=(((chip, features), BF16), ((features, features), BF16)),
        flops=2 * chip * features * (count + features),
    )

    for repeat in range(2):
        sums = sums + swap(sums, 3) + swap(sums, 5) + swap(sums, 6)
        sums = sums + swap(sums, 9)
        shapes, scratch = ((wide, F32), (part, F32)), (((chip, LANES), F32),)
        totals, *rows = call(
            functools.partial(sweep_rows, target_count),
            shapes[: 1 + repeat],
            block,
            sums,
            mass,
            scratch=scratch if repeat else shapes[1:] + scratch,
        )
        totals = (totals, swap(totals, 1), both(totals, 1), cross(totals))
        if repeat == 0:
            (sums,) = call(
                functools.partial(sweep_cols, source_count),
                ((part, F32),),
                block,
                *totals,
                target_mass,
                target_mass_far,
                scratch=(((part[0], 8, LANES), F32), ((chip, LANES), F32)),
            )
    rows, cols = call(
        functools.partial(finish, source_count),
        ((tall, F32), (flat, F32)),
        rows[0],
        swap(rows[0], 1),
        *totals,
        target_mass,
    )
    return (rows.reshape(-1), cols.reshape(-1))


def pick(mesh, plan, source):
    rows, n = mesh.shape["rows"], mesh.shape["cols"]
    features = source[1] // n
    fits = (plan[0] // rows) * (plan[1] // n) * 4 <= 4 * MIB
    even = n == 16 and features % 16 == 0
    whole = plan[0] % (rows * 1024) == 0 and plan[1] % (n * 128) == 0
    return body if rows == 2 and fits and even and whole else plain_body


def solution(mesh):
    def run(plan, source, target, source_mass, target_mass):
        chosen = pick(mesh, plan.shape, source.shape)
        return jax.shard_map(
            chosen,
            mesh=mesh,
            in_specs=(P("rows", "cols"), P("rows", "cols"), P("cols", "rows"), P("rows"), P("cols")),
            out_specs=(P("rows"), P("cols")),
            check_vma=False,
        )(plan, source, target, source_mass, target_mass)

    return run
```

```python
import functools

import jax
import jax.numpy as jnp
from jax import lax
from jax.experimental import pallas as pl
from jax.experimental.pallas import tpu as pltpu
from jax.sharding import PartitionSpec as P

sharpness = 1.5
LANES = 128
F32 = jnp.float32
BF16 = jnp.bfloat16
VMEM = pl.BlockSpec(memory_space=pltpu.VMEM)
ANY = pl.BlockSpec(memory_space=pl.ANY)
MIB = 1024 * 1024
LOG2E = 1.4426950408889634


def unit_rows(matrix):
    values = matrix.astype(F32)
    return (values * lax.rsqrt(jnp.sum(values * values, axis=1, keepdims=True) + 1e-06)).astype(
        BF16
    )


def plain_body(plan, source, target, source_mass, target_mass):
    sources_unit = unit_rows(lax.all_gather(source, "cols", axis=1, tiled=True))
    targets_unit = unit_rows(lax.all_gather(target, "rows", axis=1, tiled=True))
    projected = jnp.dot(plan, targets_unit, preferred_element_type=F32).astype(BF16)
    partial_coupling = lax.dot_general(
        sources_unit, projected, (((0,), (0,)), ((), ())), preferred_element_type=F32
    )
    coupling = lax.psum(partial_coupling, ("rows", "cols"))
    normalized = (coupling * lax.rsqrt(jnp.sum(coupling * coupling) / 2048.0 + 1e-06)).astype(BF16)
    lifted = jnp.dot(sources_unit, normalized, preferred_element_type=F32).astype(BF16)
    scores = lax.dot_general(
        lifted, targets_unit, (((1,), (1,)), ((), ())), preferred_element_type=F32
    )
    kernel = jnp.exp(sharpness * scores)
    source_count = plan.shape[0] * lax.axis_size("rows")
    target_count = plan.shape[1] * lax.axis_size("cols")
    col_scaling = jnp.ones((plan.shape[1],), F32)
    row_scaling = source_mass
    for repeat in range(2):
        row_totals = lax.psum(jnp.dot(kernel, col_scaling, precision=lax.Precision.HIGHEST), "cols")
        row_scaling = source_mass / (row_totals / target_count)
        col_totals = lax.psum(jnp.dot(row_scaling, kernel, precision=lax.Precision.HIGHEST), "rows")
        col_scaling = target_mass / (col_totals / source_count)
    return (row_scaling, col_scaling)


def square_targets(plan, near, mass, target_mass, squares, mass_out, target_mass_out):
    mass_out[...] = mass[...]
    target_mass_out[...] = target_mass[...]
    values = near[...].astype(F32)
    total = jnp.sum(values * values, axis=1, keepdims=True)
    squares[...] = jnp.broadcast_to(total, squares.shape)


def half_index():
    index = lax.axis_index("cols")
    return (index ^ (index >> 1) ^ (index >> 2) ^ (index >> 3)) & 1


def unit_targets(near, near_x, squares, units):
    a, b = near[...].astype(F32), near_x[...].astype(F32)
    inverse = lax.rsqrt(squares[:, :1] + jnp.sum(b * b, axis=1, keepdims=True) + 1e-06)
    units[:, : a.shape[1]] = (a * inverse).astype(BF16)
    units[:, a.shape[1] :] = (b * inverse).astype(BF16)


def project(start, plan, plan_far, units, units_far, out):
    height = min(512, out.shape[0])

    def step(i, _):
        at = pl.multiple_of(i * height, height)
        here = pl.ds(pl.multiple_of(start + i * height, height), height)
        total = jnp.dot(plan[here, :], units[...], preferred_element_type=F32)
        total += jnp.dot(plan_far[here, :], units_far[...], preferred_element_type=F32)
        out[pl.ds(at, height), :] = total.astype(BF16)
        return 0

    lax.fori_loop(0, out.shape[0] // height, step, 0)


def sum_squares(*refs):
    total = 0.0
    for piece in refs[:-1]:
        total += jnp.sum(piece[...].astype(F32) ** 2, axis=0, keepdims=True)
    refs[-1][...] = total


def couple(
    p0, p1, p2, p3, p4, p5, p6, p7, squares, squares_y, upper, lower,
    keep, to_x, to_y, to_xy, units,
):
    inverse = lax.rsqrt(squares[...] + squares_y[...] + 1e-06)
    rows = p0.shape[0]
    for i, piece in enumerate((p0, p1, p2, p3, p4, p5, p6, p7)):
        units[i * rows : (i + 1) * rows, :] = (piece[...].astype(F32) * inverse).astype(BF16)
    half, split = keep.shape
    part = upper.shape[0]
    product = jnp.dot(units[:, :part], upper[...], preferred_element_type=F32)
    product += jnp.dot(units[:, part:], lower[...], preferred_element_type=F32)
    keep[...] = product[:half, :split]
    to_x[...] = product[:half, split:].astype(BF16)
    to_y[...] = product[half:, :split].astype(BF16)
    to_xy[...] = product[half:, split:].astype(BF16)


def left_part(targets, targets_far, c0, x0, c1, x1, left, squares, whole):
    rows, split = c0.shape
    for i, pair in enumerate(((c0, x0), (c1, x1))):
        for j, piece in enumerate(pair):
            whole[i * rows : (i + 1) * rows, j * split : (j + 1) * split] = piece[...]
    nt = (((1,), (1,)), ((), ()))
    count = targets.shape[0]
    for i, points in enumerate((targets, targets_far)):
        product = lax.dot_general(points[...], whole[...], nt, preferred_element_type=F32)
        left[i * count : (i + 1) * count, :] = product.astype(BF16)
    squares[...] = jnp.broadcast_to(jnp.sum(whole[...].astype(F32) ** 2), squares.shape)


def kernel_block(
    left, squares, targets, targets_far, c2, x2, c3, x3, near, far,
    out, sums, left_far, squares_far, whole,
):
    left_part(targets, targets_far, c2, x2, c3, x3, left_far, squares_far, whole)
    total = squares[:1, :1] + squares_far[:1, :1]
    scale = lax.rsqrt(total / 2048.0 + 1e-06) * (sharpness * LOG2E)
    count = out.shape[1]
    width, first = min(512, count), half_index() * count
    for start in range(0, count, width):
        here = slice(start, start + width)
        there = pl.ds(pl.multiple_of(first + start, width), width)
        scores = jnp.dot(left[...], near[:, there], preferred_element_type=F32)
        scores += jnp.dot(left_far[...], far[:, there], preferred_element_type=F32)
        block = jnp.exp2(scores * scale)
        out[:, here] = block
        total = jnp.sum(block, axis=0, keepdims=True)
        for j in range(width // LANES):
            row = start // LANES + j
            sums[row : row + 1, :] = total[:, j * LANES : (j + 1) * LANES]


def sweep_rows(target_count, block, totals, mass, sums, rows, acc):
    count = rows.shape[0]
    start = pl.multiple_of(half_index() * count, count)
    rows[...] = mass[pl.ds(start, count), :] / (totals[...] / target_count)
    for start in range(0, block.shape[0], 64):
        here = slice(start, start + 64)
        total = jnp.zeros((64, LANES), F32)
        for j in range(rows.shape[0]):
            total += block[here, j * LANES : (j + 1) * LANES] * rows[j : j + 1, :]
        acc[here, :] = total
    sums[...] = jnp.sum(acc[...].T, axis=0, keepdims=True)


def chip_totals(own, core, both, x):
    count = own.shape[1] // 2
    other = core[...] + both[...]
    other = jnp.concatenate([other[:, count:], other[:, :count]], axis=1)
    return own[...] + x[...] + other


def sweep_cols(source_count, block, own, core, both, x, mass, mass_far, sums, acc, spread):
    masses = jnp.concatenate([mass[...], mass_far[...]], axis=1)
    cols = masses / (chip_totals(own, core, both, x) / source_count)
    spread[...] = jnp.broadcast_to(cols, (LANES, block.shape[0])).T
    acc[...] = jnp.zeros_like(acc)
    for start in range(0, block.shape[0], 64):
        here = slice(start, start + 64)
        for j in range(acc.shape[0]):
            part = block[here, j * LANES : (j + 1) * LANES] * spread[here, :]
            acc[j] += jnp.sum(part.reshape(8, 8, LANES), axis=0)
    sums[...] = jnp.sum(acc[...], axis=1)


def finish(source_count, rows_own, rows_far, own, core, both, x, mass, rows, cols):
    count, mine = rows_own.shape[0], half_index()
    rows[pl.ds(pl.multiple_of(mine * count, count), count), :] = rows_own[...]
    rows[pl.ds(pl.multiple_of((1 - mine) * count, count), count), :] = rows_far[...]
    totals = chip_totals(own, core, both, x)[:, : cols.shape[1]]
    cols[...] = mass[...] / (totals / source_count)


def turned(value, order):
    blocks = value.astype(F32).reshape(len(order), -1, value.shape[1])
    return jnp.concatenate([blocks[i] for i in order], axis=0)


def body(plan, source, target, source_mass, target_mass):
    n = lax.axis_size("cols")

    def swap(value, bits):
        return lax.ppermute(value, "cols", [(i, i ^ bits) for i in range(n)])

    def cross(value):
        return lax.ppermute(value, "rows", [(0, 1), (1, 0)])

    def both(value, bits):
        pairs = [(r * n + i, (1 - r) * n + (i ^ bits)) for r in range(2) for i in range(n)]
        return lax.ppermute(value, ("rows", "cols"), pairs)

    def call(function, shapes, *values, scratch=(), mib=16, flops=0, loose=()):
        outs = tuple(jax.ShapeDtypeStruct(shape, kind) for shape, kind in shapes)
        moved = sum(value.size * value.dtype.itemsize for value in values + outs)
        return pl.pallas_call(
            function,
            out_shape=outs,
            in_specs=[ANY if i in loose else VMEM for i in range(len(values))],
            out_specs=(VMEM,) * len(shapes),
            scratch_shapes=[pltpu.VMEM(shape, kind) for shape, kind in scratch],
            compiler_params=pltpu.CompilerParams(vmem_limit_bytes=mib * MIB),
            cost_estimate=pl.CostEstimate(flops=flops, bytes_accessed=moved, transcendentals=0),
        )(*values)

    hold = lax.optimization_barrier
    sources, targets = plan.shape
    target_count = targets * n
    source_count = sources * lax.axis_size("rows")
    features = source.shape[1] * n
    half = features // 4
    split = features // 2

    own = source.T
    z2, z1, y0 = swap(own, 9), swap(own, 5), swap(own, 3)
    wide, part = (targets, features), sources // 2
    target_x = cross(target)
    plan_far = swap(plan, 1)
    tall, flat = (sources // LANES, LANES), (1, targets)
    weights, mass, target_mass = call(
        square_targets,
        (((targets, LANES), F32), (tall, F32), (flat, F32)),
        plan,
        target,
        source_mass.reshape(tall),
        target_mass.reshape(flat),
        loose=(0,),
    )
    weights, y0, z1, z2 = hold((weights, y0, z1, z2))
    z3, yz2, yz1 = swap(z2, 5), swap(z2, 3), swap(y0, 5)
    target_x, z1 = hold((target_x, z1))
    (units,) = call(unit_targets, ((wide, BF16),), target, target_x, weights)
    units_far = swap(units, 1)
    (upper,) = call(
        functools.partial(project, 0),
        (((part, features), BF16),),
        plan,
        plan_far,
        units,
        units_far,
        flops=4 * part * targets * features,
    )
    target_mass_far = swap(target_mass, 1)
    upper, target_mass_far, z3 = hold((upper, target_mass_far, z3))
    yz3 = swap(z3, 3)
    near_units, yz2 = hold((units, yz2))
    (lower,) = call(
        functools.partial(project, part),
        (((part, features), BF16),),
        plan,
        plan_far,
        near_units,
        units_far,
        flops=4 * part * targets * features,
    )
    (squares,) = call(sum_squares, (((1, sources), F32),), own, z2, z1, z3)

    squares += swap(squares, 1)
    squares_y = swap(squares, 3)
    yz3, yz1, squares_y, lower = hold((yz3, yz1, squares_y, lower))
    pieces = [own, z2, z1, z3, y0, yz2, yz1, yz3]
    quarter = ((half, split), BF16)
    coupling, to_x, to_y, to_xy, xs = call(
        couple,
        (((half, split), F32), quarter, quarter, quarter, ((split, sources), BF16)),
        *pieces,
        squares,
        squares_y,
        upper,
        lower,
        flops=2 * sources * split * features,
    )
    xs_far = swap(xs, 1)

    for other in (cross(to_x), swap(to_y, 3), both(to_xy, 3)):
        coupling += other.astype(F32)
    coupling += turned(swap(coupling.astype(BF16), 5), (2, 3, 0, 1))
    coupling += turned(swap(coupling.astype(BF16), 9), (1, 0, 3, 2))
    coupling = coupling.astype(BF16)
    blocks = [coupling, cross(coupling), swap(coupling, 3), both(coupling, 3)]
    blocks += [swap(block, 1) for block in blocks]

    chip, count = 2 * targets, sources // 2
    part, wide = (count // LANES, LANES), (1, chip)
    squares_shape = ((8, LANES), F32)
    left, left_squares = call(
        left_part,
        (((chip, split), BF16), squares_shape),
        units,
        units_far,
        *blocks[:4],
        scratch=(((split, features), BF16),),
        flops=2 * chip * features * split,
    )
    block, sums = call(
        kernel_block,
        (((chip, count), F32), (part, F32)),
        left,
        left_squares,
        units,
        units_far,
        *blocks[4:],
        xs,
        xs_far,
        scratch=(((chip, split), BF16), squares_shape, ((split, features), BF16)),
        flops=2 * chip * features * (count + split),
    )

    for repeat in range(2):
        sums = sums + swap(sums, 3) + swap(sums, 5) + swap(sums, 6)
        sums = sums + swap(sums, 9)
        shapes, scratch = ((wide, F32), (part, F32)), (((chip, LANES), F32),)
        totals, *rows = call(
            functools.partial(sweep_rows, target_count),
            shapes[: 1 + repeat],
            block,
            sums,
            mass,
            scratch=scratch if repeat else shapes[1:] + scratch,
        )
        totals = (totals, swap(totals, 1), both(totals, 1), cross(totals))
        if repeat == 0:
            (sums,) = call(
                functools.partial(sweep_cols, source_count),
                ((part, F32),),
                block,
                *totals,
                target_mass,
                target_mass_far,
                scratch=(((part[0], 8, LANES), F32), ((chip, LANES), F32)),
            )
    rows, cols = call(
        functools.partial(finish, source_count),
        ((tall, F32), (flat, F32)),
        rows[0],
        swap(rows[0], 1),
        *totals,
        target_mass,
    )
    return (rows.reshape(-1), cols.reshape(-1))


def pick(mesh, plan, source):
    rows, n = mesh.shape["rows"], mesh.shape["cols"]
    features = source[1] // n
    fits = (plan[0] // rows) * (plan[1] // n) * 4 <= 4 * MIB
    even = n == 16 and features % 16 == 0
    whole = plan[0] % (rows * 1024) == 0 and plan[1] % (n * 128) == 0
    return body if rows == 2 and fits and even and whole else plain_body


def solution(mesh):
    def run(plan, source, target, source_mass, target_mass):
        chosen = pick(mesh, plan.shape, source.shape)
        return jax.shard_map(
            chosen,
            mesh=mesh,
            in_specs=(P("rows", "cols"), P("rows", "cols"), P("cols", "rows"), P("rows"), P("cols")),
            out_specs=(P("rows"), P("cols")),
            check_vma=False,
        )(plan, source, target, source_mass, target_mass)

    return run
```

```python
import functools

import jax
import jax.numpy as jnp
from jax import lax
from jax.experimental import pallas as pl
from jax.experimental.pallas import tpu as pltpu
from jax.sharding import PartitionSpec as P

sharpness = 1.5
LANES = 128
F32 = jnp.float32
BF16 = jnp.bfloat16
VMEM = pl.BlockSpec(memory_space=pltpu.VMEM)
ANY = pl.BlockSpec(memory_space=pl.ANY)
MIB = 1024 * 1024
LOG2E = 1.4426950408889634


def unit_rows(matrix):
    values = matrix.astype(F32)
    return (values * lax.rsqrt(jnp.sum(values * values, axis=1, keepdims=True) + 1e-06)).astype(
        BF16
    )


def plain_body(plan, source, target, source_mass, target_mass):
    sources_unit = unit_rows(lax.all_gather(source, "cols", axis=1, tiled=True))
    targets_unit = unit_rows(lax.all_gather(target, "rows", axis=1, tiled=True))
    projected = jnp.dot(plan, targets_unit, preferred_element_type=F32).astype(BF16)
    partial_coupling = lax.dot_general(
        sources_unit, projected, (((0,), (0,)), ((), ())), preferred_element_type=F32
    )
    coupling = lax.psum(partial_coupling, ("rows", "cols"))
    normalized = (coupling * lax.rsqrt(jnp.sum(coupling * coupling) / 2048.0 + 1e-06)).astype(BF16)
    lifted = jnp.dot(sources_unit, normalized, preferred_element_type=F32).astype(BF16)
    scores = lax.dot_general(
        lifted, targets_unit, (((1,), (1,)), ((), ())), preferred_element_type=F32
    )
    kernel = jnp.exp(sharpness * scores)
    source_count = plan.shape[0] * lax.axis_size("rows")
    target_count = plan.shape[1] * lax.axis_size("cols")
    col_scaling = jnp.ones((plan.shape[1],), F32)
    row_scaling = source_mass
    for repeat in range(2):
        row_totals = lax.psum(jnp.dot(kernel, col_scaling, precision=lax.Precision.HIGHEST), "cols")
        row_scaling = source_mass / (row_totals / target_count)
        col_totals = lax.psum(jnp.dot(row_scaling, kernel, precision=lax.Precision.HIGHEST), "rows")
        col_scaling = target_mass / (col_totals / source_count)
    return (row_scaling, col_scaling)


def square_targets(plan, near, mass, target_mass, squares, mass_out, target_mass_out):
    mass_out[...] = mass[...]
    target_mass_out[...] = target_mass[...]
    values = near[...].astype(F32)
    total = jnp.sum(values * values, axis=1, keepdims=True)
    squares[...] = jnp.broadcast_to(total, squares.shape)


def half_index():
    index = lax.axis_index("cols")
    return (index ^ (index >> 1) ^ (index >> 2) ^ (index >> 3)) & 1


def unit_targets(near, near_x, squares, units):
    a, b = near[...].astype(F32), near_x[...].astype(F32)
    inverse = lax.rsqrt(squares[:, :1] + jnp.sum(b * b, axis=1, keepdims=True) + 1e-06)
    units[:, : a.shape[1]] = (a * inverse).astype(BF16)
    units[:, a.shape[1] :] = (b * inverse).astype(BF16)


def project(start, plan, plan_far, units, units_far, out):
    height = min(512, out.shape[0])

    def step(i, _):
        at = pl.multiple_of(i * height, height)
        here = pl.ds(pl.multiple_of(start + i * height, height), height)
        total = jnp.dot(plan[here, :], units[...], preferred_element_type=F32)
        total += jnp.dot(plan_far[here, :], units_far[...], preferred_element_type=F32)
        out[pl.ds(at, height), :] = total.astype(BF16)
        return 0

    lax.fori_loop(0, out.shape[0] // height, step, 0)


def sum_squares(*refs):
    total = 0.0
    for piece in refs[:-1]:
        total += jnp.sum(piece[...].astype(F32) ** 2, axis=0, keepdims=True)
    refs[-1][...] = total


def couple(
    p0, p1, p2, p3, p4, p5, p6, p7, squares, squares_y, upper, lower,
    keep, to_x, to_y, to_xy, units,
):
    inverse = lax.rsqrt(squares[...] + squares_y[...] + 1e-06)
    rows = p0.shape[0]
    for i, piece in enumerate((p0, p1, p2, p3, p4, p5, p6, p7)):
        units[i * rows : (i + 1) * rows, :] = (piece[...].astype(F32) * inverse).astype(BF16)
    half, split = keep.shape
    part = upper.shape[0]
    product = jnp.dot(units[:, :part], upper[...], preferred_element_type=F32)
    product += jnp.dot(units[:, part:], lower[...], preferred_element_type=F32)
    keep[...] = product[:half, :split]
    to_x[...] = product[:half, split:].astype(BF16)
    to_y[...] = product[half:, :split].astype(BF16)
    to_xy[...] = product[half:, split:].astype(BF16)


def left_part(targets, targets_far, c0, x0, c1, x1, left, squares, whole):
    rows, split = c0.shape
    for i, pair in enumerate(((c0, x0), (c1, x1))):
        for j, piece in enumerate(pair):
            whole[i * rows : (i + 1) * rows, j * split : (j + 1) * split] = piece[...]
    nt = (((1,), (1,)), ((), ()))
    count = targets.shape[0]
    for i, points in enumerate((targets, targets_far)):
        product = lax.dot_general(points[...], whole[...], nt, preferred_element_type=F32)
        left[i * count : (i + 1) * count, :] = product.astype(BF16)
    squares[...] = jnp.broadcast_to(jnp.sum(whole[...].astype(F32) ** 2), squares.shape)


def kernel_block(
    left, squares, targets, targets_far, c2, x2, c3, x3, near, far,
    out, sums, left_far, squares_far, whole,
):
    left_part(targets, targets_far, c2, x2, c3, x3, left_far, squares_far, whole)
    total = squares[:1, :1] + squares_far[:1, :1]
    scale = lax.rsqrt(total / 2048.0 + 1e-06) * (sharpness * LOG2E)
    count = out.shape[1]
    width, first = min(512, count), half_index() * count
    for start in range(0, count, width):
        here = slice(start, start + width)
        there = pl.ds(pl.multiple_of(first + start, width), width)
        scores = jnp.dot(left[...], near[:, there], preferred_element_type=F32)
        scores += jnp.dot(left_far[...], far[:, there], preferred_element_type=F32)
        block = jnp.exp2(scores * scale)
        out[:, here] = block
        total = jnp.sum(block, axis=0, keepdims=True)
        for j in range(width // LANES):
            row = start // LANES + j
            sums[row : row + 1, :] = total[:, j * LANES : (j + 1) * LANES]


def sweep_rows(target_count, block, totals, mass, sums, rows, acc):
    count = rows.shape[0]
    start = pl.multiple_of(half_index() * count, count)
    rows[...] = mass[pl.ds(start, count), :] / (totals[...] / target_count)
    for start in range(0, block.shape[0], 64):
        here = slice(start, start + 64)
        total = jnp.zeros((64, LANES), F32)
        for j in range(rows.shape[0]):
            total += block[here, j * LANES : (j + 1) * LANES] * rows[j : j + 1, :]
        acc[here, :] = total
    sums[...] = jnp.sum(acc[...].T, axis=0, keepdims=True)


def last_rows(target_count, block, totals, mass, sums, rows, packed, acc):
    sweep_rows(target_count, block, totals, mass, sums, rows, acc)
    count = rows.shape[0]
    for j in range(sums.shape[1] // LANES):
        packed[j : j + 1, :] = sums[:, j * LANES : (j + 1) * LANES]
    packed[packed.shape[0] - count :, :] = rows[...]


def chip_totals(own, core, both, x):
    count = own.shape[1] // 2
    other = core + both
    other = jnp.concatenate([other[:, count:], other[:, :count]], axis=1)
    return own + x + other


def sweep_cols(source_count, block, own, core, both, x, mass, mass_far, sums, acc, spread):
    masses = jnp.concatenate([mass[...], mass_far[...]], axis=1)
    cols = masses / (chip_totals(own[...], core[...], both[...], x[...]) / source_count)
    spread[...] = jnp.broadcast_to(cols, (LANES, block.shape[0])).T
    acc[...] = jnp.zeros_like(acc)
    for start in range(0, block.shape[0], 64):
        here = slice(start, start + 64)
        for j in range(acc.shape[0]):
            part = block[here, j * LANES : (j + 1) * LANES] * spread[here, :]
            acc[j] += jnp.sum(part.reshape(8, 8, LANES), axis=0)
    sums[...] = jnp.sum(acc[...], axis=1)


def finish(source_count, rows_own, own, core, both, x, mass, rows, cols):
    count, mine = rows_own.shape[0], half_index()
    rest = core.shape[0] - count
    rows[pl.ds(pl.multiple_of(mine * count, count), count), :] = rows_own[...]
    rows[pl.ds(pl.multiple_of((1 - mine) * count, count), count), :] = core[rest:, :]
    parts = [
        jnp.concatenate([ref[j : j + 1, :] for j in range(rest)], axis=1) for ref in (core, both, x)
    ]
    totals = chip_totals(own[...], *parts)[:, : cols.shape[1]]
    cols[...] = mass[...] / (totals / source_count)


def turned(value, order):
    blocks = value.astype(F32).reshape(len(order), -1, value.shape[1])
    return jnp.concatenate([blocks[i] for i in order], axis=0)


def body(plan, source, target, source_mass, target_mass):
    n = lax.axis_size("cols")

    def swap(value, bits):
        return lax.ppermute(value, "cols", [(i, i ^ bits) for i in range(n)])

    def cross(value):
        return lax.ppermute(value, "rows", [(0, 1), (1, 0)])

    def both(value, bits):
        pairs = [(r * n + i, (1 - r) * n + (i ^ bits)) for r in range(2) for i in range(n)]
        return lax.ppermute(value, ("rows", "cols"), pairs)

    def call(function, shapes, *values, scratch=(), mib=16, flops=0, loose=()):
        outs = tuple(jax.ShapeDtypeStruct(shape, kind) for shape, kind in shapes)
        moved = sum(value.size * value.dtype.itemsize for value in values + outs)
        return pl.pallas_call(
            function,
            out_shape=outs,
            in_specs=[ANY if i in loose else VMEM for i in range(len(values))],
            out_specs=(VMEM,) * len(shapes),
            scratch_shapes=[pltpu.VMEM(shape, kind) for shape, kind in scratch],
            compiler_params=pltpu.CompilerParams(vmem_limit_bytes=mib * MIB),
            cost_estimate=pl.CostEstimate(flops=flops, bytes_accessed=moved, transcendentals=0),
        )(*values)

    hold = lax.optimization_barrier
    sources, targets = plan.shape
    target_count = targets * n
    source_count = sources * lax.axis_size("rows")
    features = source.shape[1] * n
    half = features // 4
    split = features // 2

    own = source.T
    z2, z1, y0 = swap(own, 9), swap(own, 5), swap(own, 3)
    wide, part = (targets, features), sources // 2
    target_x = cross(target)
    plan_far = swap(plan, 1)
    tall, flat = (sources // LANES, LANES), (1, targets)
    weights, mass, target_mass = call(
        square_targets,
        (((targets, LANES), F32), (tall, F32), (flat, F32)),
        plan,
        target,
        source_mass.reshape(tall),
        target_mass.reshape(flat),
        loose=(0,),
    )
    weights, y0, z1, z2 = hold((weights, y0, z1, z2))
    z3, yz2, yz1 = swap(z2, 5), swap(z2, 3), swap(y0, 5)
    target_x, z1 = hold((target_x, z1))
    (units,) = call(unit_targets, ((wide, BF16),), target, target_x, weights)
    units_far = swap(units, 1)
    (upper,) = call(
        functools.partial(project, 0),
        (((part, features), BF16),),
        plan,
        plan_far,
        units,
        units_far,
        flops=4 * part * targets * features,
    )
    target_mass_far = swap(target_mass, 1)
    upper, target_mass_far, z3 = hold((upper, target_mass_far, z3))
    yz3 = swap(z3, 3)
    near_units, yz2 = hold((units, yz2))
    (lower,) = call(
        functools.partial(project, part),
        (((part, features), BF16),),
        plan,
        plan_far,
        near_units,
        units_far,
        flops=4 * part * targets * features,
    )
    (squares,) = call(sum_squares, (((1, sources), F32),), own, z2, z1, z3)

    squares += swap(squares, 1)
    squares_y = swap(squares, 3)
    yz3, yz1, squares_y, lower = hold((yz3, yz1, squares_y, lower))
    pieces = [own, z2, z1, z3, y0, yz2, yz1, yz3]
    quarter = ((half, split), BF16)
    coupling, to_x, to_y, to_xy, xs = call(
        couple,
        (((half, split), F32), quarter, quarter, quarter, ((split, sources), BF16)),
        *pieces,
        squares,
        squares_y,
        upper,
        lower,
        flops=2 * sources * split * features,
    )
    xs_far = swap(xs, 1)

    for other in (cross(to_x), swap(to_y, 3), both(to_xy, 3)):
        coupling += other.astype(F32)
    coupling += turned(swap(coupling.astype(BF16), 5), (2, 3, 0, 1))
    coupling += turned(swap(coupling.astype(BF16), 9), (1, 0, 3, 2))
    coupling = coupling.astype(BF16)
    blocks = [coupling, cross(coupling), swap(coupling, 3), both(coupling, 3)]
    blocks += [swap(block, 1) for block in blocks]

    chip, count = 2 * targets, sources // 2
    part, wide = (count // LANES, LANES), (1, chip)
    squares_shape = ((8, LANES), F32)
    left, left_squares = call(
        left_part,
        (((chip, split), BF16), squares_shape),
        units,
        units_far,
        *blocks[:4],
        scratch=(((split, features), BF16),),
        flops=2 * chip * features * split,
    )
    block, sums = call(
        kernel_block,
        (((chip, count), F32), (part, F32)),
        left,
        left_squares,
        units,
        units_far,
        *blocks[4:],
        xs,
        xs_far,
        scratch=(((chip, split), BF16), squares_shape, ((split, features), BF16)),
        flops=2 * chip * features * (count + split),
    )

    for repeat in range(2):
        sums = sums + swap(sums, 3) + swap(sums, 5) + swap(sums, 6)
        sums = sums + swap(sums, 9)
        scratch = (((chip, LANES), F32),)
        if repeat == 0:
            (totals,) = call(
                functools.partial(sweep_rows, target_count),
                ((wide, F32),),
                block,
                sums,
                mass,
                scratch=((part, F32),) + scratch,
            )
            (sums,) = call(
                functools.partial(sweep_cols, source_count),
                ((part, F32),),
                block,
                totals,
                swap(totals, 1),
                both(totals, 1),
                cross(totals),
                target_mass,
                target_mass_far,
                scratch=(((part[0], 8, LANES), F32), ((chip, LANES), F32)),
            )
        else:
            totals, rows, packed = call(
                functools.partial(last_rows, target_count),
                ((wide, F32), (part, F32), ((chip // LANES + part[0], LANES), F32)),
                block,
                sums,
                mass,
                scratch=scratch,
            )
    rows, cols = call(
        functools.partial(finish, source_count),
        ((tall, F32), (flat, F32)),
        rows,
        totals,
        swap(packed, 1),
        both(packed, 1),
        cross(packed),
        target_mass,
    )
    return (rows.reshape(-1), cols.reshape(-1))


def pick(mesh, plan, source):
    rows, n = mesh.shape["rows"], mesh.shape["cols"]
    features = source[1] // n
    fits = (plan[0] // rows) * (plan[1] // n) * 4 <= 4 * MIB
    even = n == 16 and features % 16 == 0
    whole = plan[0] % (rows * 1024) == 0 and plan[1] % (n * 128) == 0
    return body if rows == 2 and fits and even and whole else plain_body


def solution(mesh):
    def run(plan, source, target, source_mass, target_mass):
        chosen = pick(mesh, plan.shape, source.shape)
        return jax.shard_map(
            chosen,
            mesh=mesh,
            in_specs=(P("rows", "cols"), P("rows", "cols"), P("cols", "rows"), P("rows"), P("cols")),
            out_specs=(P("rows"), P("cols")),
            check_vma=False,
        )(plan, source, target, source_mass, target_mass)

    return run
```

```python
import functools

import jax
import jax.numpy as jnp
from jax import lax
from jax.experimental import pallas as pl
from jax.experimental.pallas import tpu as pltpu
from jax.sharding import PartitionSpec as P

sharpness = 1.5
LANES = 128
F32 = jnp.float32
BF16 = jnp.bfloat16
VMEM = pl.BlockSpec(memory_space=pltpu.VMEM)
ANY = pl.BlockSpec(memory_space=pl.ANY)
MIB = 1024 * 1024
LOG2E = 1.4426950408889634


def unit_rows(matrix):
    values = matrix.astype(F32)
    return (values * lax.rsqrt(jnp.sum(values * values, axis=1, keepdims=True) + 1e-06)).astype(
        BF16
    )


def plain_body(plan, source, target, source_mass, target_mass):
    sources_unit = unit_rows(lax.all_gather(source, "cols", axis=1, tiled=True))
    targets_unit = unit_rows(lax.all_gather(target, "rows", axis=1, tiled=True))
    projected = jnp.dot(plan, targets_unit, preferred_element_type=F32).astype(BF16)
    partial_coupling = lax.dot_general(
        sources_unit, projected, (((0,), (0,)), ((), ())), preferred_element_type=F32
    )
    coupling = lax.psum(partial_coupling, ("rows", "cols"))
    normalized = (coupling * lax.rsqrt(jnp.sum(coupling * coupling) / 2048.0 + 1e-06)).astype(BF16)
    lifted = jnp.dot(sources_unit, normalized, preferred_element_type=F32).astype(BF16)
    scores = lax.dot_general(
        lifted, targets_unit, (((1,), (1,)), ((), ())), preferred_element_type=F32
    )
    kernel = jnp.exp(sharpness * scores)
    source_count = plan.shape[0] * lax.axis_size("rows")
    target_count = plan.shape[1] * lax.axis_size("cols")
    col_scaling = jnp.ones((plan.shape[1],), F32)
    row_scaling = source_mass
    for repeat in range(2):
        row_totals = lax.psum(jnp.dot(kernel, col_scaling, precision=lax.Precision.HIGHEST), "cols")
        row_scaling = source_mass / (row_totals / target_count)
        col_totals = lax.psum(jnp.dot(row_scaling, kernel, precision=lax.Precision.HIGHEST), "rows")
        col_scaling = target_mass / (col_totals / source_count)
    return (row_scaling, col_scaling)


def square_targets(plan, near, mass, target_mass, squares, mass_out, target_mass_out):
    mass_out[...] = mass[...]
    target_mass_out[...] = target_mass[...]
    values = near[...].astype(F32)
    total = jnp.sum(values * values, axis=1, keepdims=True)
    squares[...] = jnp.broadcast_to(total, squares.shape)


def half_index():
    index = lax.axis_index("cols")
    return (index ^ (index >> 1) ^ (index >> 2) ^ (index >> 3)) & 1


def unit_targets(near, near_x, squares, units):
    a, b = near[...].astype(F32), near_x[...].astype(F32)
    inverse = lax.rsqrt(squares[:, :1] + jnp.sum(b * b, axis=1, keepdims=True) + 1e-06)
    units[:, : a.shape[1]] = (a * inverse).astype(BF16)
    units[:, a.shape[1] :] = (b * inverse).astype(BF16)


def project(start, plan, plan_far, units, units_far, out):
    height = min(512, out.shape[0])

    def step(i, _):
        at = pl.multiple_of(i * height, height)
        here = pl.ds(pl.multiple_of(start + i * height, height), height)
        total = jnp.dot(plan[here, :], units[...], preferred_element_type=F32)
        total += jnp.dot(plan_far[here, :], units_far[...], preferred_element_type=F32)
        out[pl.ds(at, height), :] = total.astype(BF16)
        return 0

    lax.fori_loop(0, out.shape[0] // height, step, 0)


def sum_squares(*refs):
    total = 0.0
    for piece in refs[:-1]:
        total += jnp.sum(piece[...].astype(F32) ** 2, axis=0, keepdims=True)
    refs[-1][...] = total


def couple(
    p0, p1, p2, p3, p4, p5, p6, p7, squares, squares_y, upper, lower,
    to_x, to_y, to_xy, units,
):
    inverse = lax.rsqrt(squares[...] + squares_y[...] + 1e-06)
    rows = p0.shape[0]
    for i, piece in enumerate((p0, p1, p2, p3, p4, p5, p6, p7)):
        units[i * rows : (i + 1) * rows, :] = (piece[...].astype(F32) * inverse).astype(BF16)
    half, split = to_x.shape
    part = upper.shape[0]
    for rows, cols, out in (
        (slice(half, None), slice(None), None),
        (slice(0, half), slice(split, None), to_x),
    ):
        product = jnp.dot(units[rows, :part], upper[:, cols], preferred_element_type=F32)
        product += jnp.dot(units[rows, part:], lower[:, cols], preferred_element_type=F32)
        if out is None:
            to_y[...] = product[:, :split].astype(BF16)
            to_xy[...] = product[:, split:].astype(BF16)
        else:
            out[...] = product.astype(BF16)


def couple_own(units, upper, lower, keep):
    half, split = keep.shape
    part = upper.shape[0]
    product = jnp.dot(units[:half, :part], upper[:, :split], preferred_element_type=F32)
    product += jnp.dot(units[:half, part:], lower[:, :split], preferred_element_type=F32)
    keep[...] = product


def left_part(targets, targets_far, c0, x0, c1, x1, left, squares, whole):
    rows, split = c0.shape
    for i, pair in enumerate(((c0, x0), (c1, x1))):
        for j, piece in enumerate(pair):
            whole[i * rows : (i + 1) * rows, j * split : (j + 1) * split] = piece[...]
    nt = (((1,), (1,)), ((), ()))
    count = targets.shape[0]
    for i, points in enumerate((targets, targets_far)):
        product = lax.dot_general(points[...], whole[...], nt, preferred_element_type=F32)
        left[i * count : (i + 1) * count, :] = product.astype(BF16)
    squares[...] = jnp.broadcast_to(jnp.sum(whole[...].astype(F32) ** 2), squares.shape)


def kernel_block(
    left, squares, targets, targets_far, c2, x2, c3, x3, near, far,
    out, sums, left_far, squares_far, whole,
):
    left_part(targets, targets_far, c2, x2, c3, x3, left_far, squares_far, whole)
    total = squares[:1, :1] + squares_far[:1, :1]
    scale = lax.rsqrt(total / 2048.0 + 1e-06) * (sharpness * LOG2E)
    count = out.shape[1]
    width, first = min(512, count), half_index() * count
    for start in range(0, count, width):
        here = slice(start, start + width)
        there = pl.ds(pl.multiple_of(first + start, width), width)
        scores = jnp.dot(left[...], near[:, there], preferred_element_type=F32)
        scores += jnp.dot(left_far[...], far[:, there], preferred_element_type=F32)
        block = jnp.exp2(scores * scale)
        out[:, here] = block
        total = jnp.sum(block, axis=0, keepdims=True)
        for j in range(width // LANES):
            row = start // LANES + j
            sums[row : row + 1, :] = total[:, j * LANES : (j + 1) * LANES]


def sweep_rows(target_count, block, totals, mass, sums, rows, acc):
    count = rows.shape[0]
    start = pl.multiple_of(half_index() * count, count)
    rows[...] = mass[pl.ds(start, count), :] / (totals[...] / target_count)
    for start in range(0, block.shape[0], 64):
        here = slice(start, start + 64)
        total = jnp.zeros((64, LANES), F32)
        for j in range(rows.shape[0]):
            total += block[here, j * LANES : (j + 1) * LANES] * rows[j : j + 1, :]
        acc[here, :] = total
    sums[...] = jnp.sum(acc[...].T, axis=0, keepdims=True)


def last_rows(target_count, block, totals, mass, sums, rows, packed, acc):
    sweep_rows(target_count, block, totals, mass, sums, rows, acc)
    count = rows.shape[0]
    for j in range(sums.shape[1] // LANES):
        packed[j : j + 1, :] = sums[:, j * LANES : (j + 1) * LANES]
    packed[packed.shape[0] - count :, :] = rows[...]


def chip_totals(own, core, both, x):
    count = own.shape[1] // 2
    other = core + both
    other = jnp.concatenate([other[:, count:], other[:, :count]], axis=1)
    return own + x + other


def sweep_cols(source_count, block, own, core, both, x, mass, mass_far, sums, acc, spread):
    masses = jnp.concatenate([mass[...], mass_far[...]], axis=1)
    cols = masses / (chip_totals(own[...], core[...], both[...], x[...]) / source_count)
    spread[...] = jnp.broadcast_to(cols, (LANES, block.shape[0])).T
    acc[...] = jnp.zeros_like(acc)
    for start in range(0, block.shape[0], 64):
        here = slice(start, start + 64)
        for j in range(acc.shape[0]):
            part = block[here, j * LANES : (j + 1) * LANES] * spread[here, :]
            acc[j] += jnp.sum(part.reshape(8, 8, LANES), axis=0)
    sums[...] = jnp.sum(acc[...], axis=1)


def finish(source_count, rows_own, own, core, both, x, mass, rows, cols):
    count, mine = rows_own.shape[0], half_index()
    rest = core.shape[0] - count
    rows[pl.ds(pl.multiple_of(mine * count, count), count), :] = rows_own[...]
    rows[pl.ds(pl.multiple_of((1 - mine) * count, count), count), :] = core[rest:, :]
    parts = [
        jnp.concatenate([ref[j : j + 1, :] for j in range(rest)], axis=1) for ref in (core, both, x)
    ]
    totals = chip_totals(own[...], *parts)[:, : cols.shape[1]]
    cols[...] = mass[...] / (totals / source_count)


def turned(value, order):
    blocks = value.astype(F32).reshape(len(order), -1, value.shape[1])
    return jnp.concatenate([blocks[i] for i in order], axis=0)


def body(plan, source, target, source_mass, target_mass):
    n = lax.axis_size("cols")

    def swap(value, bits):
        return lax.ppermute(value, "cols", [(i, i ^ bits) for i in range(n)])

    def cross(value):
        return lax.ppermute(value, "rows", [(0, 1), (1, 0)])

    def both(value, bits):
        pairs = [(r * n + i, (1 - r) * n + (i ^ bits)) for r in range(2) for i in range(n)]
        return lax.ppermute(value, ("rows", "cols"), pairs)

    def call(function, shapes, *values, scratch=(), mib=16, flops=0, loose=()):
        outs = tuple(jax.ShapeDtypeStruct(shape, kind) for shape, kind in shapes)
        moved = sum(value.size * value.dtype.itemsize for value in values + outs)
        return pl.pallas_call(
            function,
            out_shape=outs,
            in_specs=[ANY if i in loose else VMEM for i in range(len(values))],
            out_specs=(VMEM,) * len(shapes),
            scratch_shapes=[pltpu.VMEM(shape, kind) for shape, kind in scratch],
            compiler_params=pltpu.CompilerParams(vmem_limit_bytes=mib * MIB),
            cost_estimate=pl.CostEstimate(flops=flops, bytes_accessed=moved, transcendentals=0),
        )(*values)

    hold = lax.optimization_barrier
    sources, targets = plan.shape
    target_count = targets * n
    source_count = sources * lax.axis_size("rows")
    features = source.shape[1] * n
    half = features // 4
    split = features // 2

    own = source.T
    z2, z1, y0 = swap(own, 9), swap(own, 5), swap(own, 3)
    wide, part = (targets, features), sources // 2
    target_x = cross(target)
    plan_far = swap(plan, 1)
    tall, flat = (sources // LANES, LANES), (1, targets)
    weights, mass, target_mass = call(
        square_targets,
        (((targets, LANES), F32), (tall, F32), (flat, F32)),
        plan,
        target,
        source_mass.reshape(tall),
        target_mass.reshape(flat),
        loose=(0,),
    )
    weights, y0, z1, z2 = hold((weights, y0, z1, z2))
    z3, yz2, yz1 = swap(z2, 5), swap(z2, 3), swap(y0, 5)
    target_x, z1 = hold((target_x, z1))
    (units,) = call(unit_targets, ((wide, BF16),), target, target_x, weights)
    units_far = swap(units, 1)
    (upper,) = call(
        functools.partial(project, 0),
        (((part, features), BF16),),
        plan,
        plan_far,
        units,
        units_far,
        flops=4 * part * targets * features,
    )
    target_mass_far = swap(target_mass, 1)
    upper, target_mass_far, z3 = hold((upper, target_mass_far, z3))
    yz3 = swap(z3, 3)
    near_units, yz2 = hold((units, yz2))
    (lower,) = call(
        functools.partial(project, part),
        (((part, features), BF16),),
        plan,
        plan_far,
        near_units,
        units_far,
        flops=4 * part * targets * features,
    )
    (squares,) = call(sum_squares, (((1, sources), F32),), own, z2, z1, z3)

    squares += swap(squares, 1)
    squares_y = swap(squares, 3)
    yz3, yz1, squares_y, lower = hold((yz3, yz1, squares_y, lower))
    pieces = [own, z2, z1, z3, y0, yz2, yz1, yz3]
    quarter = ((half, split), BF16)
    to_x, to_y, to_xy, xs = call(
        couple,
        (quarter, quarter, quarter, ((split, sources), BF16)),
        *pieces,
        squares,
        squares_y,
        upper,
        lower,
        flops=2 * sources * split * features,
    )
    (coupling,) = call(
        couple_own, (((half, split), F32),), xs, upper, lower, flops=2 * sources * half * split
    )
    xs_far = swap(xs, 1)

    for other in (cross(to_x), swap(to_y, 3), both(to_xy, 3)):
        coupling += other.astype(F32)
    coupling += turned(swap(coupling.astype(BF16), 5), (2, 3, 0, 1))
    coupling += turned(swap(coupling.astype(BF16), 9), (1, 0, 3, 2))
    coupling = coupling.astype(BF16)
    blocks = [coupling, cross(coupling), swap(coupling, 3), both(coupling, 3)]
    blocks += [swap(block, 1) for block in blocks]

    chip, count = 2 * targets, sources // 2
    part, wide = (count // LANES, LANES), (1, chip)
    squares_shape = ((8, LANES), F32)
    left, left_squares = call(
        left_part,
        (((chip, split), BF16), squares_shape),
        units,
        units_far,
        *blocks[:4],
        scratch=(((split, features), BF16),),
        flops=2 * chip * features * split,
    )
    block, sums = call(
        kernel_block,
        (((chip, count), F32), (part, F32)),
        left,
        left_squares,
        units,
        units_far,
        *blocks[4:],
        xs,
        xs_far,
        scratch=(((chip, split), BF16), squares_shape, ((split, features), BF16)),
        flops=2 * chip * features * (count + split),
    )

    for repeat in range(2):
        sums = sums + swap(sums, 3) + swap(sums, 5) + swap(sums, 6)
        sums = sums + swap(sums, 9)
        scratch = (((chip, LANES), F32),)
        if repeat == 0:
            (totals,) = call(
                functools.partial(sweep_rows, target_count),
                ((wide, F32),),
                block,
                sums,
                mass,
                scratch=((part, F32),) + scratch,
            )
            (sums,) = call(
                functools.partial(sweep_cols, source_count),
                ((part, F32),),
                block,
                totals,
                swap(totals, 1),
                both(totals, 1),
                cross(totals),
                target_mass,
                target_mass_far,
                scratch=(((part[0], 8, LANES), F32), ((chip, LANES), F32)),
            )
        else:
            totals, rows, packed = call(
                functools.partial(last_rows, target_count),
                ((wide, F32), (part, F32), ((chip // LANES + part[0], LANES), F32)),
                block,
                sums,
                mass,
                scratch=scratch,
            )
    rows, cols = call(
        functools.partial(finish, source_count),
        ((tall, F32), (flat, F32)),
        rows,
        totals,
        swap(packed, 1),
        both(packed, 1),
        cross(packed),
        target_mass,
    )
    return (rows.reshape(-1), cols.reshape(-1))


def pick(mesh, plan, source):
    rows, n = mesh.shape["rows"], mesh.shape["cols"]
    features = source[1] // n
    fits = (plan[0] // rows) * (plan[1] // n) * 4 <= 4 * MIB
    even = n == 16 and features % 16 == 0
    whole = plan[0] % (rows * 1024) == 0 and plan[1] % (n * 128) == 0
    return body if rows == 2 and fits and even and whole else plain_body


def solution(mesh):
    def run(plan, source, target, source_mass, target_mass):
        chosen = pick(mesh, plan.shape, source.shape)
        return jax.shard_map(
            chosen,
            mesh=mesh,
            in_specs=(P("rows", "cols"), P("rows", "cols"), P("cols", "rows"), P("rows"), P("cols")),
            out_specs=(P("rows"), P("cols")),
            check_vma=False,
        )(plan, source, target, source_mass, target_mass)

    return run
```

```python
import functools

import jax
import jax.numpy as jnp
from jax import lax
from jax.experimental import pallas as pl
from jax.experimental.pallas import tpu as pltpu
from jax.sharding import PartitionSpec as P

sharpness = 1.5
LANES = 128
F32 = jnp.float32
BF16 = jnp.bfloat16
VMEM = pl.BlockSpec(memory_space=pltpu.VMEM)
ANY = pl.BlockSpec(memory_space=pl.ANY)
MIB = 1024 * 1024
LOG2E = 1.4426950408889634


def unit_rows(matrix):
    values = matrix.astype(F32)
    return (values * lax.rsqrt(jnp.sum(values * values, axis=1, keepdims=True) + 1e-06)).astype(
        BF16
    )


def plain_body(plan, source, target, source_mass, target_mass):
    sources_unit = unit_rows(lax.all_gather(source, "cols", axis=1, tiled=True))
    targets_unit = unit_rows(lax.all_gather(target, "rows", axis=1, tiled=True))
    projected = jnp.dot(plan, targets_unit, preferred_element_type=F32).astype(BF16)
    partial_coupling = lax.dot_general(
        sources_unit, projected, (((0,), (0,)), ((), ())), preferred_element_type=F32
    )
    coupling = lax.psum(partial_coupling, ("rows", "cols"))
    normalized = (coupling * lax.rsqrt(jnp.sum(coupling * coupling) / 2048.0 + 1e-06)).astype(BF16)
    lifted = jnp.dot(sources_unit, normalized, preferred_element_type=F32).astype(BF16)
    scores = lax.dot_general(
        lifted, targets_unit, (((1,), (1,)), ((), ())), preferred_element_type=F32
    )
    kernel = jnp.exp(sharpness * scores)
    source_count = plan.shape[0] * lax.axis_size("rows")
    target_count = plan.shape[1] * lax.axis_size("cols")
    col_scaling = jnp.ones((plan.shape[1],), F32)
    row_scaling = source_mass
    for repeat in range(2):
        row_totals = lax.psum(jnp.dot(kernel, col_scaling, precision=lax.Precision.HIGHEST), "cols")
        row_scaling = source_mass / (row_totals / target_count)
        col_totals = lax.psum(jnp.dot(row_scaling, kernel, precision=lax.Precision.HIGHEST), "rows")
        col_scaling = target_mass / (col_totals / source_count)
    return (row_scaling, col_scaling)


def square_targets(plan, near, mass, target_mass, squares, mass_out, target_mass_out):
    mass_out[...] = mass[...]
    target_mass_out[...] = target_mass[...]
    values = near[...].astype(F32)
    total = jnp.sum(values * values, axis=1, keepdims=True)
    squares[...] = jnp.broadcast_to(total, squares.shape)


def half_index():
    index = lax.axis_index("cols")
    return (index ^ (index >> 1) ^ (index >> 2) ^ (index >> 3)) & 1


def unit_targets(near, near_x, squares, units):
    a, b = near[...].astype(F32), near_x[...].astype(F32)
    inverse = lax.rsqrt(squares[:, :1] + jnp.sum(b * b, axis=1, keepdims=True) + 1e-06)
    units[:, : a.shape[1]] = (a * inverse).astype(BF16)
    units[:, a.shape[1] :] = (b * inverse).astype(BF16)


def project(start, plan, plan_far, units, units_far, out):
    height = min(512, out.shape[0])

    def step(i, _):
        at = pl.multiple_of(i * height, height)
        here = pl.ds(pl.multiple_of(start + i * height, height), height)
        total = jnp.dot(plan[here, :], units[...], preferred_element_type=F32)
        total += jnp.dot(plan_far[here, :], units_far[...], preferred_element_type=F32)
        out[pl.ds(at, height), :] = total.astype(BF16)
        return 0

    lax.fori_loop(0, out.shape[0] // height, step, 0)


def sum_squares(*refs):
    total = 0.0
    for piece in refs[:-1]:
        total += jnp.sum(piece[...].astype(F32) ** 2, axis=0, keepdims=True)
    refs[-1][...] = total


def couple(
    p0, p1, p2, p3, p4, p5, p6, p7, squares, squares_y, upper, lower,
    to_x, to_y, to_xy, units,
):
    inverse = lax.rsqrt(squares[...] + squares_y[...] + 1e-06)
    rows = p0.shape[0]
    for i, piece in enumerate((p0, p1, p2, p3, p4, p5, p6, p7)):
        units[i * rows : (i + 1) * rows, :] = (piece[...].astype(F32) * inverse).astype(BF16)
    half, split = to_x.shape
    part = upper.shape[0]
    for rows, cols, out in (
        (slice(half, None), slice(None), None),
        (slice(0, half), slice(split, None), to_x),
    ):
        product = jnp.dot(units[rows, :part], upper[:, cols], preferred_element_type=F32)
        product += jnp.dot(units[rows, part:], lower[:, cols], preferred_element_type=F32)
        if out is None:
            to_y[...] = product[:, :split].astype(BF16)
            to_xy[...] = product[:, split:].astype(BF16)
        else:
            out[...] = product.astype(BF16)


def couple_own(units, upper, lower, keep):
    half, split = keep.shape
    part = upper.shape[0]
    product = jnp.dot(units[:half, :part], upper[:, :split], preferred_element_type=F32)
    product += jnp.dot(units[:half, part:], lower[:, :split], preferred_element_type=F32)
    keep[...] = product


def left_part(targets, targets_far, c0, x0, c1, x1, left, squares, whole):
    rows, split = c0.shape
    for i, pair in enumerate(((c0, x0), (c1, x1))):
        for j, piece in enumerate(pair):
            whole[i * rows : (i + 1) * rows, j * split : (j + 1) * split] = piece[...]
    nt = (((1,), (1,)), ((), ()))
    count = targets.shape[0]
    for i, points in enumerate((targets, targets_far)):
        product = lax.dot_general(points[...], whole[...], nt, preferred_element_type=F32)
        left[i * count : (i + 1) * count, :] = product.astype(BF16)
    squares[...] = jnp.broadcast_to(jnp.sum(whole[...].astype(F32) ** 2), squares.shape)


def kernel_block(
    left, squares, targets, targets_far, c2, x2, c3, x3, near, far,
    out, sums, left_far, squares_far, whole,
):
    left_part(targets, targets_far, c2, x2, c3, x3, left_far, squares_far, whole)
    total = squares[:1, :1] + squares_far[:1, :1]
    scale = lax.rsqrt(total / 2048.0 + 1e-06) * (sharpness * LOG2E)
    count = out.shape[1]
    width, first = min(512, count), half_index() * count
    for start in range(0, count, width):
        here = slice(start, start + width)
        there = pl.ds(pl.multiple_of(first + start, width), width)
        scores = jnp.dot(left[...], near[:, there], preferred_element_type=F32)
        scores += jnp.dot(left_far[...], far[:, there], preferred_element_type=F32)
        block = jnp.exp2(scores * scale)
        out[:, here] = block
        total = jnp.sum(block, axis=0, keepdims=True)
        for j in range(width // LANES):
            row = start // LANES + j
            sums[row : row + 1, :] = total[:, j * LANES : (j + 1) * LANES]


def sweep_rows(target_count, block, totals, more, mass, sums, rows, acc):
    count = rows.shape[0]
    start = pl.multiple_of(half_index() * count, count)
    rows[...] = mass[pl.ds(start, count), :] / ((totals[...] + more[...]) / target_count)
    for start in range(0, block.shape[0], 64):
        here = slice(start, start + 64)
        total = jnp.zeros((64, LANES), F32)
        for j in range(rows.shape[0]):
            total += block[here, j * LANES : (j + 1) * LANES] * rows[j : j + 1, :]
        acc[here, :] = total
    sums[...] = jnp.sum(acc[...].T, axis=0, keepdims=True)


def last_rows(target_count, block, totals, more, mass, sums, rows, packed, acc):
    sweep_rows(target_count, block, totals, more, mass, sums, rows, acc)
    count = rows.shape[0]
    for j in range(sums.shape[1] // LANES):
        packed[j : j + 1, :] = sums[:, j * LANES : (j + 1) * LANES]
    packed[packed.shape[0] - count :, :] = rows[...]


def chip_totals(own, core, both, x):
    count = own.shape[1] // 2
    other = core + both
    other = jnp.concatenate([other[:, count:], other[:, :count]], axis=1)
    return own + x + other


def sweep_cols(source_count, block, own, core, both, x, mass, mass_far, sums, acc, spread):
    masses = jnp.concatenate([mass[...], mass_far[...]], axis=1)
    cols = masses / (chip_totals(own[...], core[...], both[...], x[...]) / source_count)
    spread[...] = jnp.broadcast_to(cols, (LANES, block.shape[0])).T
    acc[...] = jnp.zeros_like(acc)
    for start in range(0, block.shape[0], 64):
        here = slice(start, start + 64)
        for j in range(acc.shape[0]):
            part = block[here, j * LANES : (j + 1) * LANES] * spread[here, :]
            acc[j] += jnp.sum(part.reshape(8, 8, LANES), axis=0)
    sums[...] = jnp.sum(acc[...], axis=1)


def finish(source_count, rows_own, own, core, both, x, mass, rows, cols):
    count, mine = rows_own.shape[0], half_index()
    rest = core.shape[0] - count
    rows[pl.ds(pl.multiple_of(mine * count, count), count), :] = rows_own[...]
    rows[pl.ds(pl.multiple_of((1 - mine) * count, count), count), :] = core[rest:, :]
    parts = [
        jnp.concatenate([ref[j : j + 1, :] for j in range(rest)], axis=1) for ref in (core, both, x)
    ]
    totals = chip_totals(own[...], *parts)[:, : cols.shape[1]]
    cols[...] = mass[...] / (totals / source_count)


def turned(value, order):
    blocks = value.astype(F32).reshape(len(order), -1, value.shape[1])
    return jnp.concatenate([blocks[i] for i in order], axis=0)


def body(plan, source, target, source_mass, target_mass):
    n = lax.axis_size("cols")

    def swap(value, bits):
        return lax.ppermute(value, "cols", [(i, i ^ bits) for i in range(n)])

    def cross(value):
        return lax.ppermute(value, "rows", [(0, 1), (1, 0)])

    def both(value, bits):
        pairs = [(r * n + i, (1 - r) * n + (i ^ bits)) for r in range(2) for i in range(n)]
        return lax.ppermute(value, ("rows", "cols"), pairs)

    def call(function, shapes, *values, scratch=(), mib=16, flops=0, loose=()):
        outs = tuple(jax.ShapeDtypeStruct(shape, kind) for shape, kind in shapes)
        moved = sum(value.size * value.dtype.itemsize for value in values + outs)
        return pl.pallas_call(
            function,
            out_shape=outs,
            in_specs=[ANY if i in loose else VMEM for i in range(len(values))],
            out_specs=(VMEM,) * len(shapes),
            scratch_shapes=[pltpu.VMEM(shape, kind) for shape, kind in scratch],
            compiler_params=pltpu.CompilerParams(vmem_limit_bytes=mib * MIB),
            cost_estimate=pl.CostEstimate(flops=flops, bytes_accessed=moved, transcendentals=0),
        )(*values)

    hold = lax.optimization_barrier
    sources, targets = plan.shape
    target_count = targets * n
    source_count = sources * lax.axis_size("rows")
    features = source.shape[1] * n
    half = features // 4
    split = features // 2

    own = source.T
    z2, z1, y0 = swap(own, 9), swap(own, 5), swap(own, 3)
    wide, part = (targets, features), sources // 2
    target_x = cross(target)
    plan_far = swap(plan, 1)
    tall, flat = (sources // LANES, LANES), (1, targets)
    weights, mass, target_mass = call(
        square_targets,
        (((targets, LANES), F32), (tall, F32), (flat, F32)),
        plan,
        target,
        source_mass.reshape(tall),
        target_mass.reshape(flat),
        loose=(0,),
    )
    weights, y0, z1, z2 = hold((weights, y0, z1, z2))
    z3, yz2, yz1 = swap(z2, 5), swap(z2, 3), swap(y0, 5)
    target_x, z1 = hold((target_x, z1))
    (units,) = call(unit_targets, ((wide, BF16),), target, target_x, weights)
    units_far = swap(units, 1)
    (upper,) = call(
        functools.partial(project, 0),
        (((part, features), BF16),),
        plan,
        plan_far,
        units,
        units_far,
        flops=4 * part * targets * features,
    )
    target_mass_far = swap(target_mass, 1)
    upper, target_mass_far, z3 = hold((upper, target_mass_far, z3))
    yz3 = swap(z3, 3)
    near_units, yz2 = hold((units, yz2))
    (lower,) = call(
        functools.partial(project, part),
        (((part, features), BF16),),
        plan,
        plan_far,
        near_units,
        units_far,
        flops=4 * part * targets * features,
    )
    (squares,) = call(sum_squares, (((1, sources), F32),), own, z2, z1, z3)

    squares += swap(squares, 1)
    squares_y = swap(squares, 3)
    yz3, yz1, squares_y, lower = hold((yz3, yz1, squares_y, lower))
    pieces = [own, z2, z1, z3, y0, yz2, yz1, yz3]
    quarter = ((half, split), BF16)
    to_x, to_y, to_xy, xs = call(
        couple,
        (quarter, quarter, quarter, ((split, sources), BF16)),
        *pieces,
        squares,
        squares_y,
        upper,
        lower,
        flops=2 * sources * split * features,
    )
    (coupling,) = call(
        couple_own, (((half, split), F32),), xs, upper, lower, flops=2 * sources * half * split
    )
    xs_far = swap(xs, 1)

    for other in (cross(to_x), swap(to_y, 3), both(to_xy, 3)):
        coupling += other.astype(F32)
    coupling += turned(swap(coupling.astype(BF16), 5), (2, 3, 0, 1))
    coupling += turned(swap(coupling.astype(BF16), 9), (1, 0, 3, 2))
    coupling = coupling.astype(BF16)
    blocks = [coupling, cross(coupling), swap(coupling, 3), both(coupling, 3)]
    blocks += [swap(block, 1) for block in blocks]

    chip, count = 2 * targets, sources // 2
    part, wide = (count // LANES, LANES), (1, chip)
    squares_shape = ((8, LANES), F32)
    left, left_squares = call(
        left_part,
        (((chip, split), BF16), squares_shape),
        units,
        units_far,
        *blocks[:4],
        scratch=(((split, features), BF16),),
        flops=2 * chip * features * split,
    )
    block, sums = call(
        kernel_block,
        (((chip, count), F32), (part, F32)),
        left,
        left_squares,
        units,
        units_far,
        *blocks[4:],
        xs,
        xs_far,
        scratch=(((chip, split), BF16), squares_shape, ((split, features), BF16)),
        flops=2 * chip * features * (count + split),
    )

    for repeat in range(2):
        sums = sums + swap(sums, 3) + swap(sums, 5) + swap(sums, 6)
        more = swap(sums, 9)
        scratch = (((chip, LANES), F32),)
        if repeat == 0:
            (totals,) = call(
                functools.partial(sweep_rows, target_count),
                ((wide, F32),),
                block,
                sums,
                more,
                mass,
                scratch=((part, F32),) + scratch,
            )
            (sums,) = call(
                functools.partial(sweep_cols, source_count),
                ((part, F32),),
                block,
                totals,
                swap(totals, 1),
                both(totals, 1),
                cross(totals),
                target_mass,
                target_mass_far,
                scratch=(((part[0], 8, LANES), F32), ((chip, LANES), F32)),
            )
        else:
            totals, rows, packed = call(
                functools.partial(last_rows, target_count),
                ((wide, F32), (part, F32), ((chip // LANES + part[0], LANES), F32)),
                block,
                sums,
                more,
                mass,
                scratch=scratch,
            )
    rows, cols = call(
        functools.partial(finish, source_count),
        ((tall, F32), (flat, F32)),
        rows,
        totals,
        swap(packed, 1),
        both(packed, 1),
        cross(packed),
        target_mass,
    )
    return (rows.reshape(-1), cols.reshape(-1))


def pick(mesh, plan, source):
    rows, n = mesh.shape["rows"], mesh.shape["cols"]
    features = source[1] // n
    fits = (plan[0] // rows) * (plan[1] // n) * 4 <= 4 * MIB
    even = n == 16 and features % 16 == 0
    whole = plan[0] % (rows * 1024) == 0 and plan[1] % (n * 128) == 0
    return body if rows == 2 and fits and even and whole else plain_body


def solution(mesh):
    def run(plan, source, target, source_mass, target_mass):
        chosen = pick(mesh, plan.shape, source.shape)
        return jax.shard_map(
            chosen,
            mesh=mesh,
            in_specs=(P("rows", "cols"), P("rows", "cols"), P("cols", "rows"), P("rows"), P("cols")),
            out_specs=(P("rows"), P("cols")),
            check_vma=False,
        )(plan, source, target, source_mass, target_mass)

    return run
```
